512 devices in a mesh: dp: 64 (over z, y), mp: 8 (over x, core).
Axes of the slice: x: 4, y: 4, z: 16, core: 2. Of those that a mesh axis runs over, the one named last changes fastest.
Arguments:
- tokens: bfloat16 [1024, 144, 512], P(('dp', 'mp')), may hold values from -6 to 6
- cotangent: bfloat16 [1024, 144, 512], P(('dp', 'mp')), may hold values from -6 to 6
- region_ids: int32 [1024, 144], P(('dp', 'mp')), may hold values from 0 to 3
- rel_bucket: int32 [144, 144], replicated, may hold values from 0 to 758
- norm_gain: float32 [512], replicated, may hold values from 0.5 to 1.5
- in_weight: bfloat16 [512, 1536], P('mp'), may hold values from -0.25 to 0.25
- out_weight: bfloat16 [512, 512], P('mp'), may hold values from -0.25 to 0.25
- bias_table: float32 [8, 759], replicated, may hold values from -3 to 250
- in_error: float32 [64, 512, 1536], P('dp', 'mp'), may hold values from -12 to 12
- out_error: float32 [64, 512, 512], P('dp', 'mp'), may hold values from -6 to 6
- in_basis: float32 [8, 1536, 32], P('mp'), may hold values from -6 to 6
- out_basis: float32 [8, 512, 32], P('mp'), may hold values from -6 to 6
Outputs:
- token_grad: bfloat16 [1024, 144, 512], P(('dp', 'mp'))
- gain_grad: float32 [512], replicated
- table_grad: float32 [8, 759], replicated
- in_update: float32 [512, 1536], P('mp')
- out_update: float32 [512, 512], P('mp')
- in_new_error: float32 [64, 512, 1536], P('dp', 'mp')
- out_new_error: float32 [64, 512, 512], P('dp', 'mp')
- in_new_basis: float32 [8, 1536, 32], P('mp')
- out_new_basis: float32 [8, 512, 32], P('mp')
The draws below stay inside these ranges and needn't reach their ends.
All inputs are finite; a program needn't handle non-finite values.
Results may differ from the reference program's by a relative error of at most 0.024.
Values may be sent and summed in bfloat16 or wider, within the bound.
A program may use at most 64 MiB of HBM per device.

```python
import jax
import jax.numpy as jnp
from jax import lax

D = 512
HEADS = 8
RANK = 32
WIN_DEV = 2
WT = 144
BUCKETS = 759
WINDOWS = 1024
N_DP = 64
N_MP = 8


def draw_bias_table(key, part):
    key = jax.random.fold_in(key, 7)
    base_key = jax.random.fold_in(key, 0)
    values = jnp.clip(jax.random.normal(base_key, (HEADS, BUCKETS), jnp.float32), -3.0, 3.0)
    return values


def place_ends(entries, key, smallest, largest):
    longest = entries.shape.index(max(entries.shape))
    spots = []
    for shift in (0, 1):
        where = [jax.random.randint(jax.random.fold_in(key, axis), (), 0, length) for axis, length in enumerate(entries.shape)]
        where[longest] = (where[longest] + shift) % entries.shape[longest]
        spots.append(tuple(where))
    return entries.at[spots[0]].set(smallest).at[spots[1]].set(largest)


def block_scale(rng, shape, cuts, smallest, high):
    level, own = 1.0, jax.random.fold_in(rng, 6)
    for axis_at, blocks in cuts:
        heights = jnp.exp(jax.random.uniform(jax.random.fold_in(own, axis_at), (blocks,), jnp.float32, smallest / len(cuts), high / len(cuts)))
        level = level * jnp.repeat(heights, shape[axis_at] // blocks).reshape([-1 if axis == axis_at else 1 for axis in range(len(shape))])
    return level


def gaussian(stream_key, shape, spread, reach, shards=(), held_as=jnp.bfloat16):
    drawn = spread * jax.random.normal(stream_key, shape, jnp.float32)
    if shards:
        drawn = drawn * block_scale(stream_key, shape, shards, -0.22, 0.18)
    return jnp.clip(drawn, -reach, reach).astype(held_as)


def setup_inputs(seed: int = 0) -> dict:
    key_list = jax.random.split(jax.random.key(seed), 13)
    return {
        "tokens": gaussian(key_list[0], (WINDOWS, WT, D), 1.0, 6.0, ((0, 512),)),
        "cotangent": gaussian(key_list[1], (WINDOWS, WT, D), 1.0, 6.0, ((0, 512),)),
        "region_ids": place_ends(jax.random.randint(key_list[2], (WINDOWS, WT), 0, 4), jax.random.fold_in(key_list[2], 1), 0, 3).astype(jnp.int32),
        "rel_bucket": place_ends(jax.random.randint(key_list[3], (WT, WT), 0, BUCKETS), jax.random.fold_in(key_list[3], 1), 0, BUCKETS - 1).astype(jnp.int32),
        "norm_gain": jnp.clip(1.0 + 0.1 * jax.random.normal(key_list[4], (D,), jnp.float32), 0.5, 1.5),
        "in_weight": gaussian(key_list[5], (D, 3 * D), D ** -0.5, 0.25, ((0, 8),)),
        "out_weight": gaussian(key_list[6], (D, D), D ** -0.5, 0.25, ((0, 8),)),
        "bias_table": draw_bias_table(jax.random.fold_in(key_list[12], 71), 0),
        "in_error": gaussian(key_list[8], (N_DP, D, 3 * D), 2.0, 12.0, ((0, 64), (1, 8)), jnp.float32),
        "out_error": gaussian(key_list[9], (N_DP, D, D), 1.0, 6.0, ((0, 64), (1, 8)), jnp.float32),
        "in_basis": gaussian(key_list[10], (N_MP, 3 * D, RANK), 1.0, 6.0, ((0, 8),), jnp.float32),
        "out_basis": gaussian(key_list[11], (N_MP, D, RANK), 1.0, 6.0, ((0, 8),), jnp.float32),
    }


NORM_EPS = 1e-05
BASIS_EPS = 1e-06
MASKED = -1e+30
HIGH = lax.Precision.HIGHEST

def norm_forward(token_rows):
    tokens_wide = token_rows.astype(jnp.float32)
    mean_x = lax.optimization_barrier(jnp.mean(tokens_wide, axis=-1, keepdims=True))
    centered = tokens_wide - mean_x
    variance = lax.optimization_barrier(jnp.mean(centered * centered, axis=-1, keepdims=True))
    inv_sigma = lax.rsqrt(variance + NORM_EPS)
    return (centered * inv_sigma, inv_sigma)

def orthonormal(left_factor):

    def next_column(j, finished):
        j = j.astype(jnp.int32)
        column = lax.dynamic_slice_in_dim(left_factor, j, 1, 1)
        for repeat in range(2):
            column = column - jnp.dot(finished, jnp.dot(finished.T, column, precision=HIGH), precision=HIGH)
        column = column * lax.rsqrt(jnp.sum(column * column) + BASIS_EPS)
        return lax.dynamic_update_slice_in_dim(finished, column, j, 1)
    return lax.fori_loop(0, left_factor.shape[1], next_column, jnp.zeros_like(left_factor))

def layer_grads(tokens, cotangent, region_ids, rel_bucket, norm_gain, in_weight, out_weight, bias_table):
    window_count, win_span, feature_count = tokens.shape
    head_count = bias_table.shape[0]
    head_size = feature_count // head_count
    row_count = window_count * win_span
    score_scale = head_size ** (-0.5)
    f32 = jnp.float32
    x_hat, inv_sigma = norm_forward(tokens.reshape(row_count, feature_count))
    normed = (x_hat * norm_gain).astype(jnp.bfloat16)
    projected = jnp.dot(normed, in_weight, preferred_element_type=f32).astype(jnp.bfloat16)
    projected = projected.reshape(window_count, win_span, 3, head_count, head_size)
    queries = projected[:, :, 0].astype(f32)
    key_rows = projected[:, :, 1].astype(f32)
    value_rows = projected[:, :, 2].astype(f32)
    pos_bias = jnp.take(bias_table, rel_bucket, axis=1)
    allowed = region_ids[:, :, None] == region_ids[:, None, :]
    scores = jnp.einsum('wihd,wjhd->whij', queries, key_rows) * score_scale + pos_bias[None]
    scores = jnp.where(allowed[:, None], scores, MASKED)
    row_top = lax.optimization_barrier(jnp.max(scores, axis=-1, keepdims=True))
    exp_scores = jnp.exp(scores - row_top)
    attn_prob = exp_scores / lax.optimization_barrier(jnp.sum(exp_scores, axis=-1, keepdims=True))
    prob_b = attn_prob.astype(jnp.bfloat16)
    mixed_out = jnp.einsum('whij,wjhd->wihd', prob_b.astype(f32), value_rows).astype(jnp.bfloat16)
    mixed_out = mixed_out.reshape(row_count, feature_count)
    cot_rows = cotangent.reshape(row_count, feature_count)
    out_term = jnp.dot(mixed_out.T, cot_rows, preferred_element_type=f32)
    mixed_grad = jnp.dot(cot_rows, out_weight.T, preferred_element_type=f32).astype(jnp.bfloat16)
    mixed_grad = mixed_grad.reshape(window_count, win_span, head_count, head_size).astype(f32)
    prob_grad = jnp.einsum('wihd,wjhd->whij', mixed_grad, value_rows)
    value_grad = jnp.einsum('whij,wihd->wjhd', prob_b.astype(f32), mixed_grad)
    score_grad = attn_prob * (prob_grad - lax.optimization_barrier(jnp.sum(attn_prob * prob_grad, axis=-1, keepdims=True)))
    score_sum = lax.optimization_barrier(jnp.sum(score_grad, axis=0)).reshape(head_count, win_span * win_span)
    table_term = jax.ops.segment_sum(score_sum.T, rel_bucket.reshape(-1), num_segments=bias_table.shape[1]).T
    score_b = score_grad.astype(jnp.bfloat16).astype(f32)
    query_grad = jnp.einsum('whij,wjhd->wihd', score_b, key_rows) * score_scale
    key_grad = jnp.einsum('whij,wihd->wjhd', score_b, queries) * score_scale
    packed_grad = jnp.stack([query_grad, key_grad, value_grad], axis=2).astype(jnp.bfloat16)
    packed_grad = packed_grad.reshape(row_count, 3 * feature_count)
    in_term = jnp.dot(normed.T, packed_grad, preferred_element_type=f32)
    normed_grad = jnp.dot(packed_grad, in_weight.T, preferred_element_type=f32)
    gain_term = lax.optimization_barrier(jnp.sum(normed_grad * x_hat, axis=0))
    hat_grad = normed_grad * norm_gain
    token_delta = inv_sigma * (hat_grad - lax.optimization_barrier(jnp.mean(hat_grad, axis=-1, keepdims=True)) - x_hat * lax.optimization_barrier(jnp.mean(hat_grad * x_hat, axis=-1, keepdims=True)))
    token_grad = (cot_rows.astype(f32) + token_delta).astype(jnp.bfloat16).reshape(tokens.shape)
    return (token_grad, in_term, out_term, gain_term, table_term)

def compress(group_grad, error, basis):
    row_block = group_grad.shape[1] // N_MP
    merged = (group_grad + error).reshape(N_DP, N_MP, row_block, group_grad.shape[2])
    left_factor = jnp.einsum('amrc,mck->mrk', merged, basis, precision=HIGH) / N_DP
    left_basis = jax.vmap(orthonormal)(left_factor)
    right_factor = jnp.einsum('amrc,mrk->mck', merged, left_basis, precision=HIGH) / N_DP
    update = jnp.einsum('mrk,mck->mrc', left_basis, right_factor, precision=HIGH)
    new_error = merged - update[None]
    return (update.reshape(group_grad.shape[1], group_grad.shape[2]), new_error.reshape(group_grad.shape), right_factor)

def reference(tokens, cotangent, region_ids, rel_bucket, norm_gain, in_weight, out_weight, bias_table, in_error, out_error, in_basis, out_basis):

    def blocks_of(array):
        return array.reshape((N_DP, N_MP, WIN_DEV) + array.shape[1:])

    def per_device(block):
        token_grad, in_term, out_term, gain_term, table_term = layer_grads(block[0], block[1], block[2], rel_bucket, norm_gain, in_weight, out_weight, bias_table)
        return (token_grad, in_term.astype(jnp.bfloat16), out_term.astype(jnp.bfloat16), gain_term, table_term)

    def worker(block):
        token_grad, in_terms, out_terms, gain_terms, table_terms = lax.map(per_device, block)
        in_terms = lax.optimization_barrier(in_terms)
        out_terms = lax.optimization_barrier(out_terms)
        in_group = lax.optimization_barrier(jnp.sum(in_terms.astype(jnp.float32), axis=0)) / N_MP
        out_group = lax.optimization_barrier(jnp.sum(out_terms.astype(jnp.float32), axis=0)) / N_MP
        return (token_grad, in_group, out_group, lax.optimization_barrier(jnp.sum(gain_terms, axis=0)), lax.optimization_barrier(jnp.sum(table_terms, axis=0)))
    token_grad, in_group, out_group, gain_parts, table_parts = lax.map(worker, (blocks_of(tokens), blocks_of(cotangent), blocks_of(region_ids)))
    devices = N_DP * N_MP
    gain_grad = lax.optimization_barrier(jnp.sum(gain_parts, axis=0)) / devices
    table_grad = lax.optimization_barrier(jnp.sum(table_parts, axis=0)) / devices
    in_update, in_new_error, in_new_basis = compress(in_group, in_error, in_basis)
    out_update, out_new_error, out_new_basis = compress(out_group, out_error, out_basis)
    return (token_grad.reshape(tokens.shape), gain_grad, table_grad, in_update, out_update, in_new_error, out_new_error, in_new_basis, out_new_basis)
```

```python
import functools

import jax
import jax.numpy as jnp
from jax import lax
from jax.experimental import pallas as pl
from jax.experimental.pallas import tpu as pltpu
from jax.sharding import PartitionSpec as P

NORM_EPS = 1e-05
BASIS_EPS = 1e-06
MASKED = -1e30
HIGH = lax.Precision.HIGHEST
MESH = pl.DeviceIdType.MESH
F32 = jnp.float32
BF16 = jnp.bfloat16
VMEM = pl.BlockSpec(memory_space=pltpu.VMEM)

WIN, SPAN, WIDTH, HEADS, CHUNKS = 2, 144, 512, 8, 6
ROWS = WIN * SPAN
N_X, N_Y, N_Z, N_MP = 4, 4, 16, 8
BLOCK = 64
COLS = 4 * WIDTH


def nt(a, b, **kw):
    return lax.dot_general(a, b, (((1,), (1,)), ((), ())), preferred_element_type=F32, **kw)


def tn(a, b, **kw):
    return lax.dot_general(a, b, (((0,), (0,)), ((), ())), preferred_element_type=F32, **kw)


def nn(a, b, **kw):
    return jnp.dot(a, b, preferred_element_type=F32, **kw)


def gather_kernel(in_ref, out_ref, full_in, full_out, send, recv, fsend, frecv, local):
    mp = lax.axis_index("mp")
    x, core = mp // 2, mp % 2
    sibling = {"mp": 2 * x + 1 - core}

    def peer(step):
        return {"mp": 2 * ((x + step) % N_X) + core}

    barrier = pltpu.get_barrier_semaphore()
    for target in (sibling, peer(1), peer(2), peer(3)):
        pl.semaphore_signal(barrier, inc=1, device_id=target, device_id_type=MESH)

    def rows(index):
        return pl.ds(pl.multiple_of(index * BLOCK, BLOCK), BLOCK)

    arrays = ((in_ref, full_in), (out_ref, full_out))
    own = [pltpu.make_async_copy(src, full.at[rows(mp)], local.at[k]) for k, (src, full) in enumerate(arrays)]
    for copy in own:
        copy.start()
    pl.semaphore_wait(barrier, 4)

    first = {}
    for step in (2, 1, 3):
        for k, (src, full) in enumerate(arrays):
            first[step, k] = pltpu.make_async_remote_copy(
                src, full.at[rows(mp)], send.at[k, step - 1], recv.at[k, step - 1], device_id=peer(step), device_id_type=MESH
            )
            first[step, k].start()
    forward = []
    for k, (src, full) in enumerate(arrays):
        copy = pltpu.make_async_remote_copy(
            src, full.at[rows(mp)], fsend.at[k, 0], frecv.at[k, 0], device_id=sibling, device_id_type=MESH
        )
        copy.start()
        forward.append(copy)
    for k in range(2):
        for step in (1, 3, 2):
            full = arrays[k][1]
            first[step, k].wait_recv()
            slab = full.at[rows(2 * ((x + N_X - step) % N_X) + core)]
            copy = pltpu.make_async_remote_copy(
                slab, slab, fsend.at[k, step], frecv.at[k, step], device_id=sibling, device_id_type=MESH
            )
            copy.start()
            forward.append(copy)
    for copy in own:
        copy.wait()
    for copy in first.values():
        copy.wait_send()
    for copy in forward:
        copy.wait()


def gather_weights(in_weight, out_weight):
    return pl.pallas_call(
        gather_kernel,
        out_shape=(
            jax.ShapeDtypeStruct((WIDTH, 3 * WIDTH), BF16),
            jax.ShapeDtypeStruct((WIDTH, WIDTH), BF16),
        ),
        in_specs=[VMEM, VMEM],
        out_specs=(VMEM, VMEM),
        scratch_shapes=[
            pltpu.SemaphoreType.DMA((2, 3)),
            pltpu.SemaphoreType.DMA((2, 3)),
            pltpu.SemaphoreType.DMA((2, 4)),
            pltpu.SemaphoreType.DMA((2, 4)),
            pltpu.SemaphoreType.DMA((2,)),
        ],
        compiler_params=pltpu.CompilerParams(collective_id=0, has_side_effects=True, vmem_limit_bytes=32 << 20),
        name="gather_weights",
    )(in_weight, out_weight)


def bias_kernel(table_ref, bucket_ref, bias_ref, wide):
    wide[...] = jnp.zeros_like(wide)
    wide[:, :SPAN] = bucket_ref[...]
    for part in range(2):
        lanes = 128 if part == 0 else SPAN - 128
        start = part * 128

        @pl.loop(0, SPAN // 16)
        def _(block):
            at = pl.ds(pl.multiple_of(block * 16, 16), 16)
            index = wide[at, pl.ds(start, 128)]
            low = index & 127
            chunk = index >> 7
            for head in range(HEADS):
                found = jnp.zeros((16, 128), F32)
                for c in range(CHUNKS):
                    row = jnp.broadcast_to(table_ref[head : head + 1, c * 128 : (c + 1) * 128], (16, 128))
                    found = jnp.where(chunk == c, jnp.take_along_axis(row, low, axis=1), found)
                bias_ref[head, at, start : start + lanes] = found[:, :lanes]


def bias_lookup(table, bucket):
    return pl.pallas_call(
        bias_kernel,
        out_shape=jax.ShapeDtypeStruct((HEADS, SPAN, SPAN), F32),
        in_specs=[VMEM, VMEM],
        out_specs=VMEM,
        scratch_shapes=[pltpu.VMEM((SPAN, 256), jnp.int32)],
        compiler_params=pltpu.CompilerParams(vmem_limit_bytes=32 << 20),
        name="bias_lookup",
    )(table, bucket)


def attention_kernel(
    tok_ref, cot_ref, region_ref, bucket_ref, bias_ref, gain_ref, win_ref, wout_ref,
    tokgrad_ref, term_ref, extra_ref,
    proj, mixgrad, mixed, packed, score_sum,
):
    gain = gain_ref[...]
    wide = tok_ref[...].astype(F32)
    centered = wide - jnp.mean(wide, axis=-1, keepdims=True)
    inv_sigma = lax.rsqrt(jnp.mean(centered * centered, axis=-1, keepdims=True) + NORM_EPS)
    x_hat = centered * inv_sigma
    normed = (x_hat * gain).astype(BF16)
    proj[...] = nn(normed, win_ref[...]).astype(BF16)
    mixgrad[...] = nt(cot_ref[...], wout_ref[...]).astype(BF16)

    lane = lax.broadcasted_iota(jnp.int32, (1, 128), 1)
    first_half = lane < 64
    halves = (first_half.astype(BF16), (lane >= 64).astype(BF16))
    scale = jnp.asarray(0.125, BF16)
    for w in range(WIN):
        region = region_ref[w : w + 1, :].astype(F32)
        square = jnp.broadcast_to(region, (SPAN, SPAN))
        allowed = square == square.T
        rows = slice(w * SPAN, (w + 1) * SPAN)
        for pair in range(HEADS // 2):
            at = [slice(k * WIDTH + pair * 128, k * WIDTH + (pair + 1) * 128) for k in range(3)]
            q = proj[rows, at[0]] * scale
            key = proj[rows, at[1]]
            value = proj[rows, at[2]]
            key_scaled = key * scale
            grad = mixgrad[rows, at[0]]
            parts = []
            for t in range(2):
                head = 2 * pair + t
                scores = nt(q * halves[t], key) + bias_ref[head]
                scores = jnp.where(allowed, scores, MASKED)
                exps = jnp.exp(scores - jnp.max(scores, axis=-1, keepdims=True))
                prob = exps * (1.0 / jnp.sum(exps, axis=-1, keepdims=True))
                prob_b = prob.astype(BF16)
                out = nn(prob_b, value)
                prob_grad = nt(grad * halves[t], value)
                value_grad = tn(prob_b, grad)
                score_grad = prob * (prob_grad - jnp.sum(prob * prob_grad, axis=-1, keepdims=True))
                if w == 0:
                    score_sum[head] = score_grad
                else:
                    score_sum[head] += score_grad
                score_b = score_grad.astype(BF16)
                parts.append((nn(score_b, key_scaled), tn(score_b, q), value_grad, out))
            merged = [jnp.where(first_half, a, b).astype(BF16) for a, b in zip(*parts)]
            for k in range(3):
                packed[rows, at[k]] = merged[k]
            mixed[rows, at[0]] = merged[3]

    term_ref[:, : 3 * WIDTH] = tn(normed, packed[...]).astype(BF16)
    term_ref[:, 3 * WIDTH :] = tn(mixed[...], cot_ref[...]).astype(BF16)

    normed_grad = nt(packed[...], win_ref[...])
    gain_term = jnp.sum(normed_grad * x_hat, axis=0, keepdims=True)
    hat_grad = normed_grad * gain
    delta = inv_sigma * (
        hat_grad
        - jnp.mean(hat_grad, axis=-1, keepdims=True)
        - x_hat * jnp.mean(hat_grad * x_hat, axis=-1, keepdims=True)
    )
    tokgrad_ref[...] = (cot_ref[...].astype(F32) + delta).astype(BF16)

    chunk_row = lax.broadcasted_iota(jnp.int32, (8, SPAN), 0)
    within = lax.broadcasted_iota(jnp.int32, (128, SPAN), 0)

    def add_row(i, total):
        bucket = bucket_ref[pl.ds(i, 1), :]
        chunk_is = jnp.broadcast_to(bucket >> 7, (8, SPAN)) == chunk_row
        one_hot = jnp.where(jnp.broadcast_to(bucket & 127, (128, SPAN)) == within, 1.0, 0.0).astype(BF16)
        picked = jnp.concatenate(
            [
                jnp.where(chunk_is, jnp.broadcast_to(score_sum[head, pl.ds(i, 1), :], (8, SPAN)), 0.0)
                for head in range(HEADS)
            ],
            axis=0,
        )
        high = picked.astype(BF16)
        low = (picked - high.astype(F32)).astype(BF16)
        return total + nt(jnp.concatenate([high, low], axis=0), one_hot)

    total = lax.fori_loop(0, SPAN, add_row, jnp.zeros((128, 128), F32))
    table_term = total[:64] + total[64:]
    for head in range(HEADS):
        extra_ref[head] = table_term[8 * head : 8 * head + 8]
        part = gain_term[:, 128 * (head // 2) : 128 * (head // 2 + 1)]
        if head % 2:
            part = pltpu.roll(part, 64, 1)
        extra_ref[head, 6:7, :] = part


def attention(tok, cot, region, bucket, bias, gain, full_in, full_out):
    return pl.pallas_call(
        attention_kernel,
        out_shape=(
            jax.ShapeDtypeStruct((ROWS, WIDTH), BF16),
            jax.ShapeDtypeStruct((WIDTH, COLS), BF16),
            jax.ShapeDtypeStruct((HEADS, 8, 128), F32),
        ),
        in_specs=[VMEM] * 8,
        out_specs=(VMEM, VMEM, VMEM),
        scratch_shapes=[
            pltpu.VMEM((ROWS, 3 * WIDTH), BF16),
            pltpu.VMEM((ROWS, WIDTH), BF16),
            pltpu.VMEM((ROWS, WIDTH), BF16),
            pltpu.VMEM((ROWS, 3 * WIDTH), BF16),
            pltpu.VMEM((HEADS, SPAN, SPAN), F32),
        ],
        compiler_params=pltpu.CompilerParams(vmem_limit_bytes=48 << 20),
        name="attention",
    )(tok, cot, region, bucket, bias, gain, full_in, full_out)


def scatter_kernel(
    term, extra, in_error, out_error, merged, extra_sum,
    near, near_x, mine, far, far_x, mine_x,
    s_near, r_near, s_near_x, r_near_x, s_far, r_far, s_far_x, r_far_x,
):
    mp = lax.axis_index("mp")
    x, core = mp // 2, mp % 2
    sibling = {"mp": 2 * x + 1 - core}

    def chip(step):
        return (x + step) % N_X

    def peer(step):
        return {"mp": 2 * chip(step) + core}

    barrier = pltpu.get_barrier_semaphore()
    for target in (sibling, peer(1), peer(2), peer(3)):
        pl.semaphore_signal(barrier, inc=1, device_id=target, device_id_type=MESH)
    pl.semaphore_wait(barrier, 4)

    order = (2, 1, 3, 0)
    first = {}
    for step in order:
        first[step] = (
            pltpu.make_async_remote_copy(
                term.at[chip(step), 1 - core], near.at[step], s_near.at[step], r_near.at[step],
                device_id=sibling, device_id_type=MESH,
            ),
            pltpu.make_async_remote_copy(
                extra.at[chip(step), 1 - core], near_x.at[step], s_near_x.at[step], r_near_x.at[step],
                device_id=sibling, device_id_type=MESH,
            ),
        )
        for copy in first[step]:
            copy.start()
    second = {}
    for step in order[:3]:
        for copy in first[step]:
            copy.wait_recv()
        mine[step] = (term[chip(step), core].astype(F32) + near[step].astype(F32)).astype(BF16)
        mine_x[step] = extra[chip(step), core] + near_x[step]
        second[step] = (
            pltpu.make_async_remote_copy(
                mine.at[step], far.at[step], s_far.at[step], r_far.at[step],
                device_id=peer(step), device_id_type=MESH,
            ),
            pltpu.make_async_remote_copy(
                mine_x.at[step], far_x.at[step], s_far_x.at[step], r_far_x.at[step],
                device_id=peer(step), device_id_type=MESH,
            ),
        )
        for copy in second[step]:
            copy.start()
    for copy in first[0]:
        copy.wait_recv()
    total = term[x, core].astype(F32) + near[0].astype(F32)
    total_x = extra[x, core] + near_x[0]
    for step in (1, 3, 2):
        for copy in second[step]:
            copy.wait_recv()
        total = total + far[step].astype(F32)
        total_x = total_x + far_x[step]
    total = total * (1.0 / N_MP)
    merged[:, : 3 * WIDTH] = total[:, : 3 * WIDTH] + in_error[...]
    merged[:, 3 * WIDTH :] = total[:, 3 * WIDTH :] + out_error[...]
    extra_sum[...] = total_x
    for step in order:
        for copy in first[step]:
            copy.wait_send()
    for step in order[:3]:
        for copy in second[step]:
            copy.wait_send()


def scatter_terms(term, extra, in_error, out_error):
    dma = pltpu.SemaphoreType.DMA((4,))
    return pl.pallas_call(
        scatter_kernel,
        out_shape=(jax.ShapeDtypeStruct((BLOCK, COLS), F32), jax.ShapeDtypeStruct((8, 128), F32)),
        in_specs=[VMEM] * 4,
        out_specs=(VMEM, VMEM),
        scratch_shapes=[
            pltpu.VMEM((4, BLOCK, COLS), BF16),
            pltpu.VMEM((4, 8, 128), F32),
            pltpu.VMEM((4, BLOCK, COLS), BF16),
            pltpu.VMEM((4, BLOCK, COLS), BF16),
            pltpu.VMEM((4, 8, 128), F32),
            pltpu.VMEM((4, 8, 128), F32),
        ]
        + [dma] * 8,
        compiler_params=pltpu.CompilerParams(collective_id=1, has_side_effects=True, vmem_limit_bytes=32 << 20),
        name="scatter_terms",
    )(term.reshape(N_X, 2, BLOCK, COLS), extra.reshape(N_X, 2, 8, 128), in_error, out_error)


def mean_kernel(
    merged, extra, mean, extra_all,
    y_in, z_in, slab, piece, extra_y, ex_y_in, ex_z_in, ex_part, ex_out,
    s_y, r_y, s_z, r_z, s_zz, r_zz, s_yy, r_yy,
    s_xy, r_xy, s_xz, r_xz, s_xyy, r_xyy, s_xm, r_xm,
):
    dp = lax.axis_index("dp")
    mp = lax.axis_index("mp")
    z, y = dp // N_Y, dp % N_Y

    def y_peer(step):
        return {"dp": z * N_Y + (y + step) % N_Y}

    def z_peer(step):
        return {"dp": ((z + step) % N_Z) * N_Y + y}

    def mp_peer(step):
        return {"mp": (mp + step) % N_MP}

    def remote(src, dst, send, recv, target):
        copy = pltpu.make_async_remote_copy(src, dst, send, recv, device_id=target, device_id_type=MESH)
        copy.start()
        return copy

    barrier = pltpu.get_barrier_semaphore()
    peers = [y_peer(s) for s in range(1, N_Y)] + [z_peer(s) for s in range(1, N_Z)] + [mp_peer(s) for s in range(1, N_MP)]
    for target in peers:
        pl.semaphore_signal(barrier, inc=1, device_id=target, device_id_type=MESH)
    for k in range(N_Y):
        extra_y[k] = extra[2 * k : 2 * k + 2, :]
    pl.semaphore_wait(barrier, len(peers))

    def slab_rows(index):
        return pl.ds(pl.multiple_of(index * 16, 16), 16)

    def piece_cols(index):
        return pl.ds(pl.multiple_of(index * 128, 128), 128)

    y_steps = (2, 1, 3)
    sends = []
    y_copies, ex_y = {}, {}
    for step in y_steps:
        other = (y + step) % N_Y
        ex_y[step] = remote(extra_y.at[other], ex_y_in.at[step], s_xy.at[step], r_xy.at[step], y_peer(step))
        y_copies[step] = remote(merged.at[slab_rows(other)], y_in.at[step], s_y.at[step], r_y.at[step], y_peer(step))
    part = extra_y[y]
    for step in y_steps:
        ex_y[step].wait_recv()
        part = part + ex_y_in[step]
    ex_part[...] = part
    z_steps = (8, 7, 9, 6, 10, 5, 11, 4, 12, 3, 13, 2, 14, 1, 15)
    ex_z = {s: remote(ex_part, ex_z_in.at[s], s_xz.at[s], r_xz.at[s], z_peer(s)) for s in z_steps}
    total = merged[slab_rows(y), :]
    for step in (1, 3, 2):
        y_copies[step].wait_recv()
        total = total + y_in[step]
    for k in range(N_Z):
        slab[k] = total[:, 128 * k : 128 * (k + 1)]

    z_copies = {s: remote(slab.at[(z + s) % N_Z], z_in.at[s], s_z.at[s], r_z.at[s], z_peer(s)) for s in z_steps}
    for step in reversed(z_steps):
        ex_z[step].wait_recv()
        part = part + ex_z_in[step]
    ex_out[y] = part
    ex_yy = {s: remote(ex_out.at[y], ex_out.at[y], s_xyy.at[s], r_xyy.at[s], y_peer(s)) for s in y_steps}
    own = slab[z]
    for step in reversed(z_steps):
        z_copies[step].wait_recv()
        own = own + z_in[step]
    piece[...] = own * (1.0 / (N_Y * N_Z))

    here = mean.at[slab_rows(y), piece_cols(z)]
    zz = {s: remote(piece, here, s_zz.at[s], r_zz.at[s], z_peer(s)) for s in z_steps}
    mean[slab_rows(y), piece_cols(z)] = piece[...]
    for step in y_steps:
        ex_yy[step].wait()
    for k in range(N_Y):
        extra_all[mp, 2 * k : 2 * k + 2, :] = ex_out[k]
    xm = {
        s: remote(extra_all.at[mp], extra_all.at[mp], s_xm.at[s], r_xm.at[s], mp_peer(s)) for s in range(1, N_MP)
    }
    for step in reversed(z_steps):
        zz[step].wait_recv()
    mine = mean.at[slab_rows(y)]
    yy = {s: remote(mine, mine, s_yy.at[s], r_yy.at[s], y_peer(s)) for s in y_steps}
    for copies in (y_copies, ex_y, z_copies, ex_z, zz):
        for copy in copies.values():
            copy.wait_send()
    for copies in (xm, yy):
        for copy in copies.values():
            copy.wait()


def mean_over_workers(merged, extra):
    def dma(n):
        return [pltpu.SemaphoreType.DMA((n,))] * 2

    return pl.pallas_call(
        mean_kernel,
        out_shape=(jax.ShapeDtypeStruct((BLOCK, COLS), F32), jax.ShapeDtypeStruct((N_MP, 8, 128), F32)),
        in_specs=[VMEM] * 2,
        out_specs=(VMEM, VMEM),
        scratch_shapes=[
            pltpu.VMEM((N_Y, 16, COLS), F32),
            pltpu.VMEM((N_Z, 16, 128), F32),
            pltpu.VMEM((N_Z, 16, 128), F32),
            pltpu.VMEM((16, 128), F32),
            pltpu.VMEM((N_Y, 2, 128), F32),
            pltpu.VMEM((N_Y, 2, 128), F32),
            pltpu.VMEM((N_Z, 2, 128), F32),
            pltpu.VMEM((2, 128), F32),
            pltpu.VMEM((N_Y, 2, 128), F32),
        ]
        + dma(N_Y) + dma(N_Z) + dma(N_Z) + dma(N_Y)
        + dma(N_Y) + dma(N_Z) + dma(N_Y) + dma(N_MP),
        compiler_params=pltpu.CompilerParams(collective_id=2, has_side_effects=True, vmem_limit_bytes=32 << 20),
        name="mean_over_workers",
    )(merged, extra)


def factor_kernel(
    mean, merged, in_basis, out_basis, in_update, out_update, in_error, out_error, in_right, out_right, left
):
    split = 3 * WIDTH
    left[:, :BLOCK] = nt(in_basis[...], mean[:, :split], precision=HIGH)
    left[:, BLOCK:] = nt(out_basis[...], mean[:, split:], precision=HIGH)

    lane = lax.broadcasted_iota(jnp.int32, (8, 128), 1)
    row = lax.broadcasted_iota(jnp.int32, (8, 128), 0)
    is_in = lane < BLOCK

    def half_sums(a):
        in_sum = jnp.sum(jnp.where(is_in, a, 0.0), axis=1, keepdims=True)
        out_sum = jnp.sum(jnp.where(is_in, 0.0, a), axis=1, keepdims=True)
        return jnp.where(is_in, in_sum, out_sum)

    finished = []
    for c in range(32):
        column = jnp.broadcast_to(left[c : c + 1, :], (8, 128))
        if c:
            for _ in range(2):
                taken = None
                for group in finished:
                    term = group * half_sums(group * column)
                    taken = term if taken is None else taken + term
                column = column - jnp.sum(taken, axis=0, keepdims=True)
        column = column * lax.rsqrt(half_sums(column * column) + BASIS_EPS)
        if c % 8 == 0:
            finished.append(jnp.where(row == 0, column, 0.0))
        else:
            finished[-1] = jnp.where(row == c % 8, column, finished[-1])
    ortho = jnp.concatenate(finished, axis=0)
    in_ortho, out_ortho = ortho[:, :BLOCK], ortho[:, BLOCK:]
    right = nn(in_ortho, mean[:, :split], precision=HIGH)
    in_right[...] = right
    update = tn(in_ortho, right, precision=HIGH)
    in_update[...] = update
    in_error[...] = merged[:, :split] - update
    right = nn(out_ortho, mean[:, split:], precision=HIGH)
    out_right[...] = right
    update = tn(out_ortho, right, precision=HIGH)
    out_update[...] = update
    out_error[...] = merged[:, split:] - update


def factors(mean, merged, in_basis, out_basis):
    wide = jax.ShapeDtypeStruct((BLOCK, 3 * WIDTH), F32)
    thin = jax.ShapeDtypeStruct((BLOCK, WIDTH), F32)
    return pl.pallas_call(
        factor_kernel,
        out_shape=(
            wide, thin, wide, thin,
            jax.ShapeDtypeStruct((32, 3 * WIDTH), F32),
            jax.ShapeDtypeStruct((32, WIDTH), F32),
        ),
        in_specs=[VMEM] * 4,
        out_specs=(VMEM,) * 6,
        scratch_shapes=[pltpu.VMEM((32, 128), F32)],
        compiler_params=pltpu.CompilerParams(vmem_limit_bytes=32 << 20),
        name="factors",
    )(mean, merged, in_basis, out_basis)


def shards(
    tokens,
    cotangent,
    region_ids,
    rel_bucket,
    norm_gain,
    in_weight,
    out_weight,
    bias_table,
    in_error,
    out_error,
    in_basis,
    out_basis,
):
    devices = lax.axis_size("dp") * lax.axis_size("mp")
    buckets = bias_table.shape[1]
    full_in, full_out = gather_weights(in_weight, out_weight)
    table = jnp.pad(bias_table, ((0, 0), (0, CHUNKS * 128 - buckets)))
    bias = bias_lookup(table, rel_bucket)
    token_grad, term, extra = attention(
        tokens.reshape(ROWS, WIDTH), cotangent.reshape(ROWS, WIDTH), region_ids, rel_bucket, bias,
        norm_gain.reshape(1, WIDTH), full_in, full_out,
    )
    merged, extra_sum = scatter_terms(term, extra, in_error[0], out_error[0])
    mean, extra_all = mean_over_workers(merged, extra_sum)
    in_update, out_update, in_new, out_new, in_right, out_right = factors(
        mean, merged, in_basis[0].T, out_basis[0].T
    )
    extra_all = extra_all * (1.0 / devices)
    gain_grad = extra_all[:, 6, :64].reshape(WIDTH)
    table_grad = extra_all[:, :CHUNKS, :].reshape(HEADS, CHUNKS * 128)[:, :buckets]
    return (
        token_grad.reshape(tokens.shape),
        gain_grad,
        table_grad,
        in_update,
        out_update,
        in_new[None],
        out_new[None],
        in_right.T[None],
        out_right.T[None],
    )


def solution(mesh):
    placed = (
        P(("dp", "mp"), None, None),
        P(("dp", "mp"), None, None),
        P(("dp", "mp"), None),
        P(),
        P(),
        P("mp", None),
        P("mp", None),
        P(),
        P("dp", "mp", None),
        P("dp", "mp", None),
        P("mp", None, None),
        P("mp", None, None),
    )
    return jax.shard_map(
        shards,
        mesh=mesh,
        in_specs=placed,
        out_specs=(
            P(("dp", "mp"), None, None),
            P(),
            P(),
            P("mp", None),
            P("mp", None),
            P("dp", "mp", None),
            P("dp", "mp", None),
            P("mp", None, None),
            P("mp", None, None),
        ),
        check_vma=False,
    )
```

```python
import functools

import jax
import jax.numpy as jnp
from jax import lax
from jax.experimental import pallas as pl
from jax.experimental.pallas import tpu as pltpu
from jax.sharding import PartitionSpec as P

NORM_EPS = 1e-05
BASIS_EPS = 1e-06
MASKED = -1e30
HIGH = lax.Precision.HIGHEST
MESH = pl.DeviceIdType.MESH
F32 = jnp.float32
BF16 = jnp.bfloat16
VMEM = pl.BlockSpec(memory_space=pltpu.VMEM)

WIN, SPAN, WIDTH, HEADS, CHUNKS = 2, 144, 512, 8, 6
ROWS = WIN * SPAN
N_X, N_Y, N_Z, N_MP = 4, 4, 16, 8
BLOCK = 64
COLS = 4 * WIDTH


def nt(a, b, **kw):
    return lax.dot_general(a, b, (((1,), (1,)), ((), ())), preferred_element_type=F32, **kw)


def tn(a, b, **kw):
    return lax.dot_general(a, b, (((0,), (0,)), ((), ())), preferred_element_type=F32, **kw)


def nn(a, b, **kw):
    return jnp.dot(a, b, preferred_element_type=F32, **kw)


def gather_kernel(in_ref, out_ref, full_in, full_out, send, recv, fsend, frecv, local):
    mp = lax.axis_index("mp")
    x, core = mp // 2, mp % 2
    sibling = {"mp": 2 * x + 1 - core}

    def peer(step):
        return {"mp": 2 * ((x + step) % N_X) + core}

    barrier = pltpu.get_barrier_semaphore()
    for target in (sibling, peer(1), peer(2), peer(3)):
        pl.semaphore_signal(barrier, inc=1, device_id=target, device_id_type=MESH)

    def rows(index):
        return pl.ds(pl.multiple_of(index * BLOCK, BLOCK), BLOCK)

    arrays = ((in_ref, full_in), (out_ref, full_out))
    own = [pltpu.make_async_copy(src, full.at[rows(mp)], local.at[k]) for k, (src, full) in enumerate(arrays)]
    for copy in own:
        copy.start()
    pl.semaphore_wait(barrier, 4)

    first = {}
    for step in (2, 1, 3):
        for k, (src, full) in enumerate(arrays):
            first[step, k] = pltpu.make_async_remote_copy(
                src, full.at[rows(mp)], send.at[k, step - 1], recv.at[k, step - 1], device_id=peer(step), device_id_type=MESH
            )
            first[step, k].start()
    forward = []
    for k, (src, full) in enumerate(arrays):
        copy = pltpu.make_async_remote_copy(
            src, full.at[rows(mp)], fsend.at[k, 0], frecv.at[k, 0], device_id=sibling, device_id_type=MESH
        )
        copy.start()
        forward.append(copy)
    for k in range(2):
        for step in (1, 3, 2):
            full = arrays[k][1]
            first[step, k].wait_recv()
            slab = full.at[rows(2 * ((x + N_X - step) % N_X) + core)]
            copy = pltpu.make_async_remote_copy(
                slab, slab, fsend.at[k, step], frecv.at[k, step], device_id=sibling, device_id_type=MESH
            )
            copy.start()
            forward.append(copy)
    for copy in own:
        copy.wait()
    for copy in first.values():
        copy.wait_send()
    for copy in forward:
        copy.wait()


def gather_weights(in_weight, out_weight):
    return pl.pallas_call(
        gather_kernel,
        out_shape=(
            jax.ShapeDtypeStruct((WIDTH, 3 * WIDTH), BF16),
            jax.ShapeDtypeStruct((WIDTH, WIDTH), BF16),
        ),
        in_specs=[VMEM, VMEM],
        out_specs=(VMEM, VMEM),
        scratch_shapes=[
            pltpu.SemaphoreType.DMA((2, 3)),
            pltpu.SemaphoreType.DMA((2, 3)),
            pltpu.SemaphoreType.DMA((2, 4)),
            pltpu.SemaphoreType.DMA((2, 4)),
            pltpu.SemaphoreType.DMA((2,)),
        ],
        compiler_params=pltpu.CompilerParams(collective_id=0, has_side_effects=True, vmem_limit_bytes=32 << 20),
        name="gather_weights",
    )(in_weight, out_weight)


def bias_kernel(table_ref, bucket_ref, bias_ref, wide):
    wide[...] = jnp.zeros_like(wide)
    wide[:, :SPAN] = bucket_ref[...]
    for part in range(2):
        lanes = 128 if part == 0 else SPAN - 128
        start = part * 128

        @pl.loop(0, SPAN // 16)
        def _(block):
            at = pl.ds(pl.multiple_of(block * 16, 16), 16)
            index = wide[at, pl.ds(start, 128)]
            low = index & 127
            chunk = index >> 7
            for head in range(HEADS):
                found = jnp.zeros((16, 128), F32)
                for c in range(CHUNKS):
                    row = jnp.broadcast_to(table_ref[head : head + 1, c * 128 : (c + 1) * 128], (16, 128))
                    found = jnp.where(chunk == c, jnp.take_along_axis(row, low, axis=1), found)
                bias_ref[head, at, start : start + lanes] = found[:, :lanes]


def bias_lookup(table, bucket):
    return pl.pallas_call(
        bias_kernel,
        out_shape=jax.ShapeDtypeStruct((HEADS, SPAN, SPAN), F32),
        in_specs=[VMEM, VMEM],
        out_specs=VMEM,
        scratch_shapes=[pltpu.VMEM((SPAN, 256), jnp.int32)],
        compiler_params=pltpu.CompilerParams(vmem_limit_bytes=32 << 20),
        name="bias_lookup",
    )(table, bucket)


def layer_kernel(
    tok_ref, cot_ref, region_ref, bucket_ref, bias_ref, gain_ref, win_ref, wout_ref, in_error, out_error,
    tokgrad_ref, merged, mean, extra_all,
    proj, mixgrad, mixed, packed, normed, x_hat, score_high, score_low,
    prod, near, mine, far,
    err_y, err_slab, err_z, err_full,
    sum_src, sum_y, sum_slab, sum_z, sum_full,
    ex, ex_near, ex_mine, ex_far, ex_part, ex_y, ex_z,
    s_near, r_near, s_far, r_far,
    s_ey, r_ey, s_ez, r_ez, s_ezz, r_ezz, s_eyy, r_eyy,
    s_ty, r_ty, s_tz, r_tz, s_tzz, r_tzz, s_tyy, r_tyy,
    s_xn, r_xn, s_xf, r_xf, s_xy, r_xy, s_xz, r_xz, s_xx, r_xx, s_xs, r_xs,
):
    dp, mp = lax.axis_index("dp"), lax.axis_index("mp")
    z, y, x, core = dp // N_Y, dp % N_Y, mp // 2, mp % 2
    sibling = {"mp": 2 * x + 1 - core}
    split = 3 * WIDTH

    def x_peer(step):
        return {"mp": 2 * ((x + step) % N_X) + core}

    def y_peer(step):
        return {"dp": z * N_Y + (y + step) % N_Y}

    def z_peer(step):
        return {"dp": ((z + step) % N_Z) * N_Y + y}

    sent = []

    def remote(src, dst, send, recv, target):
        copy = pltpu.make_async_remote_copy(src, dst, send, recv, device_id=target, device_id_type=MESH)
        copy.start()
        sent.append(copy)
        return copy

    def slab_rows(index):
        return pl.ds(pl.multiple_of(index * 16, 16), 16)

    four = (2, 1, 3)
    z_steps = (8, 7, 9, 6, 10, 5, 11, 4, 12, 3, 13, 2, 14, 1, 15)
    near_first = tuple(reversed(z_steps))

    barrier = pltpu.get_barrier_semaphore()
    peers = [z_peer(s) for s in z_steps] + [y_peer(s) for s in four] + [x_peer(s) for s in four] + [sibling]
    for target in peers:
        pl.semaphore_signal(barrier, inc=1, device_id=target, device_id_type=MESH)

    gain = gain_ref[...]
    wide = tok_ref[...].astype(F32)
    centered = wide - jnp.mean(wide, axis=-1, keepdims=True)
    inv_sigma = lax.rsqrt(jnp.mean(centered * centered, axis=-1, keepdims=True) + NORM_EPS)
    x_hat[...] = centered * inv_sigma
    normed[...] = (x_hat[...] * gain).astype(BF16)
    proj[...] = nn(normed[...], win_ref[...]).astype(BF16)
    mixgrad[...] = nt(cot_ref[...], wout_ref[...]).astype(BF16)

    pl.semaphore_wait(barrier, len(peers))

    e_y = []
    for s in four:
        rows = slab_rows((y + s) % N_Y)
        e_y.append(remote(in_error.at[rows], err_y.at[s, :, pl.ds(0, split)], s_ey.at[s, 0], r_ey.at[s, 0], y_peer(s)))
        e_y.append(
            remote(out_error.at[rows], err_y.at[s, :, pl.ds(split, WIDTH)], s_ey.at[s, 1], r_ey.at[s, 1], y_peer(s))
        )

    lane = lax.broadcasted_iota(jnp.int32, (1, 128), 1)
    first_half = lane < 64
    halves = (first_half.astype(BF16), (lane >= 64).astype(BF16))
    scale = jnp.asarray(0.125, BF16)
    allowed = []
    for w in range(WIN):
        square = jnp.broadcast_to(region_ref[w : w + 1, :].astype(F32), (SPAN, SPAN))
        allowed.append(square == square.T)

    @pl.loop(0, HEADS // 2)
    def _(pair):
        at = [pl.ds(pl.multiple_of(k * WIDTH + pair * 128, 128), 128) for k in range(3)]
        grads = [[], []]
        for w in range(WIN):
            rows = pl.ds(w * SPAN, SPAN)
            q = proj[rows, at[0]] * scale
            key = proj[rows, at[1]]
            value = proj[rows, at[2]]
            key_scaled = key * scale
            grad = mixgrad[rows, at[0]]
            parts = []
            for t in range(2):
                scores = nt(q * halves[t], key) + bias_ref[2 * pair + t]
                scores = jnp.where(allowed[w], scores, MASKED)
                exps = jnp.exp(scores - jnp.max(scores, axis=-1, keepdims=True))
                prob = exps * (1.0 / jnp.sum(exps, axis=-1, keepdims=True))
                prob_b = prob.astype(BF16)
                out = nn(prob_b, value)
                prob_grad = nt(grad * halves[t], value)
                value_grad = tn(prob_b, grad)
                score_grad = prob * (prob_grad - jnp.sum(prob * prob_grad, axis=-1, keepdims=True))
                grads[t].append(score_grad)
                score_b = score_grad.astype(BF16)
                parts.append((nn(score_b, key_scaled), tn(score_b, q), value_grad, out))
            joined = [jnp.where(first_half, a, b).astype(BF16) for a, b in zip(*parts)]
            for k in range(3):
                packed[rows, at[k]] = joined[k]
            mixed[rows, at[0]] = joined[3]
        for t in range(2):
            total = grads[t][0] + grads[t][1]
            high = total.astype(BF16).astype(F32)
            score_high[2 * pair + t] = high
            score_low[2 * pair + t] = total - high

    first = {}
    for s in (2, 1, 3, 0):
        cols = pl.ds(pl.multiple_of(((x + s) % N_X) * 128, 128), 128)
        prod[s, :, :split] = tn(normed[:, cols], packed[...]).astype(BF16)
        prod[s, :, split:] = tn(mixed[:, cols], cot_ref[...]).astype(BF16)
        other = pl.ds(pl.multiple_of((1 - core) * BLOCK, BLOCK), BLOCK)
        first[s] = remote(prod.at[s, other], near.at[s], s_near.at[s], r_near.at[s], sibling)
    own = pl.ds(pl.multiple_of(core * BLOCK, BLOCK), BLOCK)
    second = {}

    def send_second(s, c):
        rows = slab_rows((y + c) % N_Y)
        second[s, c] = remote(mine.at[s, rows], far.at[s, rows], s_far.at[s, c], r_far.at[s, c], x_peer(s))

    for s in four:
        first[s].wait_recv()
        mine[s] = (prod[s, own].astype(F32) + near[s].astype(F32)).astype(BF16)
        if s == 2:
            for c in (2, 1, 3, 0):
                send_second(s, c)
    for c in (2, 1, 3, 0):
        send_second(1, c)
        send_second(3, c)
    first[0].wait_recv()
    merged[...] = prod[0, own].astype(F32) + near[0].astype(F32)

    for copy in e_y:
        copy.wait_recv()
    err = err_y[1] + err_y[2] + err_y[3]
    err_in = err[:, :split] + in_error[slab_rows(y), :]
    err_out = err[:, split:] + out_error[slab_rows(y), :]
    for k in range(N_Z):
        src = err_in if k < 12 else err_out
        err_slab[k] = src[:, 128 * (k % 12) : 128 * (k % 12) + 128]
    e_z = {s: remote(err_slab.at[(z + s) % N_Z], err_z.at[s], s_ez.at[s], r_ez.at[s], z_peer(s)) for s in z_steps}

    normed_grad = nt(packed[...], win_ref[...])
    gain_term = jnp.sum(normed_grad * x_hat[...], axis=0, keepdims=True)
    hat_grad = normed_grad * gain
    delta = inv_sigma * (
        hat_grad
        - jnp.mean(hat_grad, axis=-1, keepdims=True)
        - x_hat[...] * jnp.mean(hat_grad * x_hat[...], axis=-1, keepdims=True)
    )
    tokgrad_ref[...] = (cot_ref[...].astype(F32) + delta).astype(BF16)

    chunk_row = lax.broadcasted_iota(jnp.int32, (8, SPAN), 0)
    within = lax.broadcasted_iota(jnp.int32, (128, SPAN), 0)

    def add_rows(block, total):
        for k in range(8):
            i = block * 8 + k
            bucket = bucket_ref[pl.ds(i, 1), :]
            chunk_is = jnp.broadcast_to(bucket >> 7, (8, SPAN)) == chunk_row
            one_hot = jnp.where(jnp.broadcast_to(bucket & 127, (128, SPAN)) == within, 1.0, 0.0).astype(BF16)
            picked = jnp.concatenate(
                [
                    jnp.where(chunk_is, jnp.broadcast_to(part[head, pl.ds(i, 1), :], (8, SPAN)), 0.0)
                    for part in (score_high, score_low)
                    for head in range(HEADS)
                ],
                axis=0,
            ).astype(BF16)
            total = total + nt(picked, one_hot)
        return total

    total = lax.fori_loop(0, SPAN // 8, add_rows, jnp.zeros((128, 128), F32))
    table_term = total[:64] + total[64:]
    for head in range(HEADS):
        ex[head // 2, head % 2] = table_term[8 * head : 8 * head + 8]
        part = gain_term[:, 128 * (head // 2) : 128 * (head // 2 + 1)]
        if head % 2:
            part = pltpu.roll(part, 64, 1)
        ex[head // 2, head % 2, 6:7, :] = part
    x_near = {
        s: remote(ex.at[(x + s) % N_X, 1 - core], ex_near.at[s], s_xn.at[s], r_xn.at[s], sibling) for s in (2, 1, 3, 0)
    }

    piece = err_slab[z]
    for s in near_first:
        e_z[s].wait_recv()
        piece = piece + err_z[s]
    err_full[y, z] = piece * (1.0 / (N_Y * N_Z))
    here = err_full.at[y, z]
    e_zz = {s: remote(here, here, s_ezz.at[s], r_ezz.at[s], z_peer(s)) for s in z_steps}

    t_y = {}
    x_far = {}
    for c in (2, 1, 3, 0):
        rows = slab_rows((y + c) % N_Y)
        for s in (1, 3, 2):
            second[s, c].wait_recv()
        total = merged[rows, :] + far[1, rows].astype(F32) + far[3, rows].astype(F32) + far[2, rows].astype(F32)
        total = total * (1.0 / N_MP)
        merged[rows, :split] = total[:, :split] + in_error[rows, :]
        merged[rows, split:] = total[:, split:] + out_error[rows, :]
        if c:
            sum_src[rows, :] = total.astype(BF16)
            t_y[c] = remote(sum_src.at[rows], sum_y.at[c], s_ty.at[c], r_ty.at[c], y_peer(c))
        if c == 2:
            for s in four:
                x_near[s].wait_recv()
                ex_mine[s] = ex[(x + s) % N_X, core] + ex_near[s]
                x_far[s] = remote(ex_mine.at[s], ex_far.at[s], s_xf.at[s], r_xf.at[s], x_peer(s))
    for s in four:
        t_y[s].wait_recv()
        total = total + sum_y[s].astype(F32)
    for k in range(N_Z):
        sum_slab[k] = total[:, 128 * k : 128 * (k + 1)]
    rounded = sum_slab[...].astype(BF16)
    sum_send = sum_full.at[N_Y]
    sum_full[N_Y] = rounded
    t_z = {s: remote(sum_send.at[(z + s) % N_Z], sum_z.at[s], s_tz.at[s], r_tz.at[s], z_peer(s)) for s in z_steps}

    x_near[0].wait_recv()
    part = ex[x, core] + ex_near[0]
    for s in four:
        x_far[s].wait_recv()
        part = part + ex_far[s]
    ex_part[0] = part
    x_y = {s: remote(ex_part.at[0], ex_y.at[s], s_xy.at[s], r_xy.at[s], y_peer(s)) for s in four}

    for s in near_first:
        e_zz[s].wait_recv()
    here = err_full.at[y]
    e_yy = {s: remote(here, here, s_eyy.at[s], r_eyy.at[s], y_peer(s)) for s in four}

    piece = sum_slab[z]
    for s in near_first:
        t_z[s].wait_recv()
        piece = piece + sum_z[s].astype(F32)
    sum_full[y, z] = (piece * (1.0 / (N_Y * N_Z))).astype(BF16)
    here = sum_full.at[y, z]
    t_zz = {s: remote(here, here, s_tzz.at[s], r_tzz.at[s], z_peer(s)) for s in z_steps}

    for s in four:
        x_y[s].wait_recv()
        part = part + ex_y[s]
    ex_part[1] = part
    x_z = {s: remote(ex_part.at[1], ex_z.at[s], s_xz.at[s], r_xz.at[s], z_peer(s)) for s in z_steps}

    for s in near_first:
        t_zz[s].wait_recv()
    here = sum_full.at[y]
    t_yy = {s: remote(here, here, s_tyy.at[s], r_tyy.at[s], y_peer(s)) for s in four}

    for s in near_first:
        x_z[s].wait_recv()
        part = part + ex_z[s]
    extra_all[mp] = part
    here = extra_all.at[mp]
    x_x = {s: remote(here, here, s_xx.at[s], r_xx.at[s], x_peer(s)) for s in four}
    x_s = [remote(here, here, s_xs.at[0], r_xs.at[0], sibling)]

    def finish(slab):
        for k in range(N_Z):
            mean[slab_rows(slab), 128 * k : 128 * (k + 1)] = err_full[slab, k] + sum_full[slab, k].astype(F32)

    finish(y)
    for s in (1, 3, 2):
        x_x[s].wait_recv()
        here = extra_all.at[2 * ((x + N_X - s) % N_X) + core]
        x_s.append(remote(here, here, s_xs.at[s], r_xs.at[s], sibling))
    for s in (1, 3, 2):
        e_yy[s].wait_recv()
        t_yy[s].wait_recv()
        finish((y + N_Y - s) % N_Y)
    for copy in x_s:
        copy.wait_recv()
    for copy in sent:
        copy.wait_send()


def layer(*operands):
    def vmem(*shape, dtype=F32):
        return pltpu.VMEM(shape, dtype)

    def dma(*shape):
        return [pltpu.SemaphoreType.DMA(shape)] * 2

    return pl.pallas_call(
        layer_kernel,
        out_shape=(
            jax.ShapeDtypeStruct((ROWS, WIDTH), BF16),
            jax.ShapeDtypeStruct((BLOCK, COLS), F32),
            jax.ShapeDtypeStruct((BLOCK, COLS), F32),
            jax.ShapeDtypeStruct((N_MP, 8, 128), F32),
        ),
        in_specs=[VMEM] * len(operands),
        out_specs=(VMEM,) * 4,
        scratch_shapes=[
            vmem(ROWS, 3 * WIDTH, dtype=BF16),
            vmem(ROWS, WIDTH, dtype=BF16),
            vmem(ROWS, WIDTH, dtype=BF16),
            vmem(ROWS, 3 * WIDTH, dtype=BF16),
            vmem(ROWS, WIDTH, dtype=BF16),
            vmem(ROWS, WIDTH),
            vmem(HEADS, SPAN, SPAN),
            vmem(HEADS, SPAN, SPAN),
            vmem(N_X, 2 * BLOCK, COLS, dtype=BF16),
            vmem(N_X, BLOCK, COLS, dtype=BF16),
            vmem(N_X, BLOCK, COLS, dtype=BF16),
            vmem(N_X, BLOCK, COLS, dtype=BF16),
            vmem(N_Y, 16, COLS),
            vmem(N_Z, 16, 128),
            vmem(N_Z, 16, 128),
            vmem(N_Y, N_Z, 16, 128),
            vmem(BLOCK, COLS, dtype=BF16),
            vmem(N_Y, 16, COLS, dtype=BF16),
            vmem(N_Z, 16, 128),
            vmem(N_Z, 16, 128, dtype=BF16),
            vmem(N_Y + 1, N_Z, 16, 128, dtype=BF16),
            vmem(N_X, 2, 8, 128),
            vmem(N_X, 8, 128),
            vmem(N_X, 8, 128),
            vmem(N_X, 8, 128),
            vmem(2, 8, 128),
            vmem(N_Y, 8, 128),
            vmem(N_Z, 8, 128),
        ]
        + dma(4) + dma(4, 4)
        + dma(4, 2) + dma(N_Z) + dma(N_Z) + dma(4)
        + dma(4) + dma(N_Z) + dma(N_Z) + dma(4)
        + dma(4) + dma(4) + dma(4) + dma(N_Z) + dma(4) + dma(4),
        compiler_params=pltpu.CompilerParams(collective_id=1, has_side_effects=True, vmem_limit_bytes=48 << 20),
        name="layer",
    )(*operands)


def factor_kernel(
    mean, merged, in_basis, out_basis, in_update, out_update, in_error, out_error, in_right, out_right, left
):
    split = 3 * WIDTH
    left[:, :BLOCK] = nt(in_basis[...], mean[:, :split], precision=HIGH)
    left[:, BLOCK:] = nt(out_basis[...], mean[:, split:], precision=HIGH)

    lane = lax.broadcasted_iota(jnp.int32, (8, 128), 1)
    row = lax.broadcasted_iota(jnp.int32, (8, 128), 0)
    is_in = lane < BLOCK

    def half_sums(a):
        in_sum = jnp.sum(jnp.where(is_in, a, 0.0), axis=1, keepdims=True)
        out_sum = jnp.sum(jnp.where(is_in, 0.0, a), axis=1, keepdims=True)
        return jnp.where(is_in, in_sum, out_sum)

    finished = []
    for c in range(32):
        column = jnp.broadcast_to(left[c : c + 1, :], (8, 128))
        if c:
            for _ in range(2):
                taken = None
                for group in finished:
                    term = group * half_sums(group * column)
                    taken = term if taken is None else taken + term
                column = column - jnp.sum(taken, axis=0, keepdims=True)
        column = column * lax.rsqrt(half_sums(column * column) + BASIS_EPS)
        if c % 8 == 0:
            finished.append(jnp.where(row == 0, column, 0.0))
        else:
            finished[-1] = jnp.where(row == c % 8, column, finished[-1])
    ortho = jnp.concatenate(finished, axis=0)
    in_ortho, out_ortho = ortho[:, :BLOCK], ortho[:, BLOCK:]
    right = nn(in_ortho, mean[:, :split], precision=HIGH)
    in_right[...] = right
    update = tn(in_ortho, right, precision=HIGH)
    in_update[...] = update
    in_error[...] = merged[:, :split] - update
    right = nn(out_ortho, mean[:, split:], precision=HIGH)
    out_right[...] = right
    update = tn(out_ortho, right, precision=HIGH)
    out_update[...] = update
    out_error[...] = merged[:, split:] - update


def factors(mean, merged, in_basis, out_basis):
    wide = jax.ShapeDtypeStruct((BLOCK, 3 * WIDTH), F32)
    thin = jax.ShapeDtypeStruct((BLOCK, WIDTH), F32)
    return pl.pallas_call(
        factor_kernel,
        out_shape=(
            wide, thin, wide, thin,
            jax.ShapeDtypeStruct((32, 3 * WIDTH), F32),
            jax.ShapeDtypeStruct((32, WIDTH), F32),
        ),
        in_specs=[VMEM] * 4,
        out_specs=(VMEM,) * 6,
        scratch_shapes=[pltpu.VMEM((32, 128), F32)],
        compiler_params=pltpu.CompilerParams(vmem_limit_bytes=32 << 20),
        name="factors",
    )(mean, merged, in_basis, out_basis)


def shards(
    tokens,
    cotangent,
    region_ids,
    rel_bucket,
    norm_gain,
    in_weight,
    out_weight,
    bias_table,
    in_error,
    out_error,
    in_basis,
    out_basis,
):
    devices = lax.axis_size("dp") * lax.axis_size("mp")
    buckets = bias_table.shape[1]
    full_in, full_out = gather_weights(in_weight, out_weight)
    table = jnp.pad(bias_table, ((0, 0), (0, CHUNKS * 128 - buckets)))
    bias = bias_lookup(table, rel_bucket)
    token_grad, merged, mean, extra_all = layer(
        tokens.reshape(ROWS, WIDTH), cotangent.reshape(ROWS, WIDTH), region_ids, rel_bucket, bias,
        norm_gain.reshape(1, WIDTH), full_in, full_out, in_error[0], out_error[0],
    )
    in_update, out_update, in_new, out_new, in_right, out_right = factors(
        mean, merged, in_basis[0].T, out_basis[0].T
    )
    extra_all = extra_all * (1.0 / devices)
    gain_grad = extra_all[:, 6, :64].reshape(WIDTH)
    table_grad = extra_all[:, :CHUNKS, :].reshape(HEADS, CHUNKS * 128)[:, :buckets]
    return (
        token_grad.reshape(tokens.shape),
        gain_grad,
        table_grad,
        in_update,
        out_update,
        in_new[None],
        out_new[None],
        in_right.T[None],
        out_right.T[None],
    )


def solution(mesh):
    placed = (
        P(("dp", "mp"), None, None),
        P(("dp", "mp"), None, None),
        P(("dp", "mp"), None),
        P(),
        P(),
        P("mp", None),
        P("mp", None),
        P(),
        P("dp", "mp", None),
        P("dp", "mp", None),
        P("mp", None, None),
        P("mp", None, None),
    )
    return jax.shard_map(
        shards,
        mesh=mesh,
        in_specs=placed,
        out_specs=(
            P(("dp", "mp"), None, None),
            P(),
            P(),
            P("mp", None),
            P("mp", None),
            P("dp", "mp", None),
            P("dp", "mp", None),
            P("mp", None, None),
            P("mp", None, None),
        ),
        check_vma=False,
    )
```

```python
import jax
import jax.numpy as jnp
from jax import lax
from jax.experimental import pallas as pl
from jax.experimental.pallas import tpu as pltpu
from jax.sharding import PartitionSpec as P

NORM_EPS = 1e-05
BASIS_EPS = 1e-06
MASKED = -1e30
HIGH = lax.Precision.HIGHEST
MESH = pl.DeviceIdType.MESH
F32 = jnp.float32
BF16 = jnp.bfloat16
VMEM = pl.BlockSpec(memory_space=pltpu.VMEM)
HBM = pl.BlockSpec(memory_space=pltpu.HBM)

WIN, SPAN, WIDTH, HEADS, CHUNKS = 2, 144, 512, 8, 6
ROWS = WIN * SPAN
N_X, N_Y, N_Z, N_MP = 4, 4, 16, 8
BLOCK = 64
COLS = 4 * WIDTH


def nt(a, b, **kw):
    return lax.dot_general(a, b, (((1,), (1,)), ((), ())), preferred_element_type=F32, **kw)


def tn(a, b, **kw):
    return lax.dot_general(a, b, (((0,), (0,)), ((), ())), preferred_element_type=F32, **kw)


def nn(a, b, **kw):
    return jnp.dot(a, b, preferred_element_type=F32, **kw)


def gather_kernel(
    in_ref, out_ref, table_hbm, bucket_hbm, tok_hbm, gain_hbm,
    full_in, full_out, bias_ref, normed_ref,
    table_ref, bucket_ref, tok_ref, gain_ref, index, table, send, recv, rsend, rrecv, fsend, frecv, local,
):
    mp = lax.axis_index("mp")
    x, core = mp // 2, mp % 2
    sibling = {"mp": 2 * x + 1 - core}

    def device(step):
        return 2 * ((x + step) % N_X) + core

    right, left = {"mp": device(1)}, {"mp": device(3)}
    barrier = pltpu.get_barrier_semaphore()
    for target in (right, left, sibling):
        pl.semaphore_signal(barrier, inc=1, device_id=target, device_id_type=MESH)

    sources, fulls = (in_ref, out_ref), (full_in, full_out)
    half_rows = BLOCK // 2

    def rows(owner):
        return pl.ds(pl.multiple_of(owner * BLOCK, BLOCK), BLOCK)

    def half(owner, h):
        return pl.ds(pl.multiple_of(owner * BLOCK + h * half_rows, half_rows), half_rows)

    own = [pltpu.make_async_copy(sources[k], fulls[k].at[rows(mp)], local.at[k]) for k in range(2)]
    staged = [
        pltpu.make_async_copy(src, dst, local.at[2 + k])
        for k, (src, dst) in enumerate(
            ((table_hbm, table_ref), (bucket_hbm, bucket_ref), (tok_hbm, tok_ref), (gain_hbm, gain_ref))
        )
    ]
    for copy in staged + own:
        copy.start()
    for copy in staged:
        copy.wait()
    index[...] = jnp.zeros_like(index)
    index[:, :SPAN] = bucket_ref[...]
    table[...] = jnp.zeros_like(table)
    table[:, : table_ref.shape[1]] = table_ref[...]
    pl.semaphore_wait(barrier, 3)

    started = []

    def remote(src, dst, send_sem, recv_sem, target):
        copy = pltpu.make_async_remote_copy(src, dst, send_sem, recv_sem, device_id=target, device_id_type=MESH)
        copy.start()
        started.append(copy)
        return copy

    first = {}
    for turn in range(2):
        for k in range(2):
            for way, target in ((0, right), (1, left)):
                h = turn ^ way
                first[way, k, h] = remote(
                    sources[k].at[pl.ds(h * half_rows, half_rows)], fulls[k].at[half(mp, h)],
                    send.at[way, k, h], recv.at[way, k, h], target,
                )
    passed = [
        remote(sources[k], fulls[k].at[rows(mp)], fsend.at[0, k, 0], frecv.at[0, k, 0], sibling) for k in range(2)
    ]

    def look_up(part):
        lanes = 128 if part == 0 else SPAN - 128

        @pl.loop(0, SPAN // 16)
        def _(block):
            at = pl.ds(pl.multiple_of(block * 16, 16), 16)
            bucket = index[at, pl.ds(part * 128, 128)]
            low = bucket & 127
            chunk = bucket >> 7
            for head in range(HEADS):
                found = jnp.zeros((16, 128), F32)
                for c in range(CHUNKS):
                    row = jnp.broadcast_to(table[head : head + 1, c * 128 : (c + 1) * 128], (16, 128))
                    found = jnp.where(chunk == c, jnp.take_along_axis(row, low, axis=1), found)
                bias_ref[head, at, part * 128 : part * 128 + lanes] = found[:, :lanes]

    def to_sibling(group, k, h, owner):
        slab = fulls[k].at[half(owner, h)]
        passed.append(remote(slab, slab, fsend.at[group, k, h], frecv.at[group, k, h], sibling))

    look_up(0)
    relayed = {}
    for k in range(2):
        for way, target in ((0, right), (1, left)):
            h = way
            first[way, k, h].wait_recv()
            owner = device(3 if way == 0 else 1)
            slab = fulls[k].at[half(owner, h)]
            relayed[way, k] = remote(slab, slab, rsend.at[way, k], rrecv.at[way, k], target)
            to_sibling(1 + way, k, h, owner)
    look_up(1)
    wide = tok_ref[...].astype(F32)
    centered = wide - jnp.mean(wide, axis=-1, keepdims=True)
    inv_sigma = lax.rsqrt(jnp.mean(centered * centered, axis=-1, keepdims=True) + NORM_EPS)
    normed_ref[...] = (centered * inv_sigma * gain_ref[...]).astype(BF16)
    for k in range(2):
        for way in range(2):
            first[way, k, 1 - way].wait_recv()
            to_sibling(1 + way, k, 1 - way, device(3 if way == 0 else 1))
    for k in range(2):
        for way in range(2):
            relayed[way, k].wait_recv()
            to_sibling(3, k, way, device(2))
    for copy in own:
        copy.wait()
    for copy in passed:
        copy.wait_recv()
    for copy in started:
        copy.wait_send()


def gather_weights(*operands):
    def dma(*shape):
        return [pltpu.SemaphoreType.DMA(shape)] * 2

    return pl.pallas_call(
        gather_kernel,
        out_shape=(
            jax.ShapeDtypeStruct((WIDTH, 3 * WIDTH), BF16),
            jax.ShapeDtypeStruct((WIDTH, WIDTH), BF16),
            jax.ShapeDtypeStruct((HEADS, SPAN, SPAN), F32),
            jax.ShapeDtypeStruct((ROWS, WIDTH), BF16),
        ),
        in_specs=[HBM] * len(operands),
        out_specs=(VMEM,) * 4,
        scratch_shapes=[pltpu.VMEM(a.shape, a.dtype) for a in operands[2:]]
        + [pltpu.VMEM((SPAN, 256), jnp.int32), pltpu.VMEM((HEADS, CHUNKS * 128), F32)]
        + dma(2, 2, 2) + dma(2, 2) + dma(4, 2, 2)
        + [pltpu.SemaphoreType.DMA((6,))],
        compiler_params=pltpu.CompilerParams(collective_id=0, has_side_effects=True, vmem_limit_bytes=32 << 20),
        name="gather_weights",
    )(*(pltpu.with_memory_space_constraint(a, pltpu.HBM) for a in operands))


def layer_kernel(
    cot_hbm, region_hbm, in_error_hbm, out_error_hbm, tok_hbm, gain_hbm, bucket_hbm,
    bias_ref, normed, win_ref, wout_ref,
    tokgrad_ref, merged, mean, extra_all,
    cot_ref, region_ref, in_error, out_error, tok_ref, gain_ref, bucket_ref, staging,
    proj, mixgrad, mixed, packed, x_hat, score_high, score_low,
    prod, near, mine, far,
    err_y, err_slab, err_z, err_full,
    sum_src, sum_y, sum_slab, sum_z, sum_full,
    ex, ex_near, ex_mine, ex_far, ex_part, ex_y, ex_z,
    s_near, r_near, s_far, r_far,
    s_ey, r_ey, s_ez, r_ez, s_ezz, r_ezz, s_eyy, r_eyy,
    s_ty, r_ty, s_tz, r_tz, s_tzz, r_tzz, s_tyy, r_tyy,
    s_xn, r_xn, s_xf, r_xf, s_xy, r_xy, s_xz, r_xz, s_xx, r_xx, s_xs, r_xs,
):
    dp, mp = lax.axis_index("dp"), lax.axis_index("mp")
    z, y, x, core = dp // N_Y, dp % N_Y, mp // 2, mp % 2
    sibling = {"mp": 2 * x + 1 - core}
    split = 3 * WIDTH

    def x_peer(step):
        return {"mp": 2 * ((x + step) % N_X) + core}

    def y_peer(step):
        return {"dp": z * N_Y + (y + step) % N_Y}

    def z_peer(step):
        return {"dp": ((z + step) % N_Z) * N_Y + y}

    sent = []

    def remote(src, dst, send, recv, target):
        copy = pltpu.make_async_remote_copy(src, dst, send, recv, device_id=target, device_id_type=MESH)
        copy.start()
        sent.append(copy)
        return copy

    def slab_rows(index):
        return pl.ds(pl.multiple_of(index * 16, 16), 16)

    four = (2, 1, 3)
    z_steps = (8, 7, 9, 6, 10, 5, 11, 4, 12, 3, 13, 2, 14, 1, 15)
    near_first = tuple(reversed(z_steps))

    barrier = pltpu.get_barrier_semaphore()
    peers = [z_peer(s) for s in z_steps] + [y_peer(s) for s in four] + [x_peer(s) for s in four] + [sibling]
    for target in peers:
        pl.semaphore_signal(barrier, inc=1, device_id=target, device_id_type=MESH)

    staged = [
        pltpu.make_async_copy(src, dst, staging.at[k])
        for k, (src, dst) in enumerate(
            (
                (cot_hbm, cot_ref), (region_hbm, region_ref), (in_error_hbm, in_error), (out_error_hbm, out_error),
                (tok_hbm, tok_ref), (gain_hbm, gain_ref), (bucket_hbm, bucket_ref),
            )
        )
    ]
    for copy in staged:
        copy.start()

    proj[...] = nn(normed[...], win_ref[...]).astype(BF16)
    for copy in staged:
        copy.wait()
    mixgrad[...] = nt(cot_ref[...], wout_ref[...]).astype(BF16)

    lane = lax.broadcasted_iota(jnp.int32, (1, 128), 1)
    first_half = lane < 64
    halves = (first_half.astype(BF16), (lane >= 64).astype(BF16))
    scale = jnp.asarray(0.125, BF16)
    allowed = []
    for w in range(WIN):
        square = jnp.broadcast_to(region_ref[w : w + 1, :].astype(F32), (SPAN, SPAN))
        allowed.append(square == square.T)

    @pl.loop(0, HEADS // 2)
    def _(pair):
        at = [pl.ds(pl.multiple_of(k * WIDTH + pair * 128, 128), 128) for k in range(3)]
        grads = [[], []]
        for w in range(WIN):
            rows = pl.ds(w * SPAN, SPAN)
            q = proj[rows, at[0]] * scale
            key = proj[rows, at[1]]
            value = proj[rows, at[2]]
            key_scaled = key * scale
            grad = mixgrad[rows, at[0]]
            parts = []
            for t in range(2):
                scores = nt(q * halves[t], key) + bias_ref[2 * pair + t]
                scores = jnp.where(allowed[w], scores, MASKED)
                exps = jnp.exp(scores - jnp.max(scores, axis=-1, keepdims=True))
                prob = exps * (1.0 / jnp.sum(exps, axis=-1, keepdims=True))
                prob_b = prob.astype(BF16)
                out = nn(prob_b, value)
                prob_grad = nt(grad * halves[t], value)
                value_grad = tn(prob_b, grad)
                score_grad = prob * (prob_grad - jnp.sum(prob * prob_grad, axis=-1, keepdims=True))
                grads[t].append(score_grad)
                score_b = score_grad.astype(BF16)
                parts.append((nn(score_b, key_scaled), tn(score_b, q), value_grad, out))
            joined = [jnp.where(first_half, a, b).astype(BF16) for a, b in zip(*parts)]
            for k in range(3):
                packed[rows, at[k]] = joined[k]
            mixed[rows, at[0]] = joined[3]
        for t in range(2):
            total = grads[t][0] + grads[t][1]
            high = total.astype(BF16).astype(F32)
            score_high[2 * pair + t] = high
            score_low[2 * pair + t] = total - high

    pl.semaphore_wait(barrier, len(peers))

    e_y = []
    for s in four:
        rows = slab_rows((y + s) % N_Y)
        e_y.append(remote(in_error.at[rows], err_y.at[s, :, pl.ds(0, split)], s_ey.at[s, 0], r_ey.at[s, 0], y_peer(s)))
        e_y.append(
            remote(out_error.at[rows], err_y.at[s, :, pl.ds(split, WIDTH)], s_ey.at[s, 1], r_ey.at[s, 1], y_peer(s))
        )

    first = {}
    for s in (2, 1, 3, 0):
        cols = pl.ds(pl.multiple_of(((x + s) % N_X) * 128, 128), 128)
        prod[s, :, :split] = tn(normed[:, cols], packed[...]).astype(BF16)
        prod[s, :, split:] = tn(mixed[:, cols], cot_ref[...]).astype(BF16)
        other = pl.ds(pl.multiple_of((1 - core) * BLOCK, BLOCK), BLOCK)
        first[s] = remote(prod.at[s, other], near.at[s], s_near.at[s], r_near.at[s], sibling)
    own = pl.ds(pl.multiple_of(core * BLOCK, BLOCK), BLOCK)
    second = {}

    def send_second(s, c):
        rows = slab_rows((y + c) % N_Y)
        second[s, c] = remote(mine.at[s, rows], far.at[s, rows], s_far.at[s, c], r_far.at[s, c], x_peer(s))

    for s in four:
        first[s].wait_recv()
        mine[s] = (prod[s, own].astype(F32) + near[s].astype(F32)).astype(BF16)
        if s == 2:
            for c in (2, 1, 3, 0):
                send_second(s, c)
    for c in (2, 1, 3, 0):
        send_second(1, c)
        send_second(3, c)
    first[0].wait_recv()
    merged[...] = prod[0, own].astype(F32) + near[0].astype(F32)

    for copy in e_y:
        copy.wait_recv()
    err = err_y[1] + err_y[2] + err_y[3]
    err_in = err[:, :split] + in_error[slab_rows(y), :]
    err_out = err[:, split:] + out_error[slab_rows(y), :]
    for k in range(N_Z):
        src = err_in if k < 12 else err_out
        err_slab[k] = src[:, 128 * (k % 12) : 128 * (k % 12) + 128]
    e_z = {s: remote(err_slab.at[(z + s) % N_Z], err_z.at[s], s_ez.at[s], r_ez.at[s], z_peer(s)) for s in z_steps}

    gain = gain_ref[...]
    wide = tok_ref[...].astype(F32)
    centered = wide - jnp.mean(wide, axis=-1, keepdims=True)
    inv_sigma = lax.rsqrt(jnp.mean(centered * centered, axis=-1, keepdims=True) + NORM_EPS)
    x_hat[...] = centered * inv_sigma
    normed_grad = nt(packed[...], win_ref[...])
    gain_term = jnp.sum(normed_grad * x_hat[...], axis=0, keepdims=True)
    hat_grad = normed_grad * gain
    delta = inv_sigma * (
        hat_grad
        - jnp.mean(hat_grad, axis=-1, keepdims=True)
        - x_hat[...] * jnp.mean(hat_grad * x_hat[...], axis=-1, keepdims=True)
    )
    tokgrad_ref[...] = (cot_ref[...].astype(F32) + delta).astype(BF16)

    chunk_row = lax.broadcasted_iota(jnp.int32, (8, SPAN), 0)
    within = lax.broadcasted_iota(jnp.int32, (128, SPAN), 0)

    def add_rows(block, total):
        for k in range(8):
            i = block * 8 + k
            bucket = bucket_ref[pl.ds(i, 1), :]
            chunk_is = jnp.broadcast_to(bucket >> 7, (8, SPAN)) == chunk_row
            one_hot = jnp.where(jnp.broadcast_to(bucket & 127, (128, SPAN)) == within, 1.0, 0.0).astype(BF16)
            picked = jnp.concatenate(
                [
                    jnp.where(chunk_is, jnp.broadcast_to(part[head, pl.ds(i, 1), :], (8, SPAN)), 0.0)
                    for part in (score_high, score_low)
                    for head in range(HEADS)
                ],
                axis=0,
            ).astype(BF16)
            total = total + nt(picked, one_hot)
        return total

    total = lax.fori_loop(0, SPAN // 8, add_rows, jnp.zeros((128, 128), F32))
    table_term = total[:64] + total[64:]
    for head in range(HEADS):
        ex[head // 2, head % 2] = table_term[8 * head : 8 * head + 8]
        part = gain_term[:, 128 * (head // 2) : 128 * (head // 2 + 1)]
        if head % 2:
            part = pltpu.roll(part, 64, 1)
        ex[head // 2, head % 2, 6:7, :] = part
    x_near = {
        s: remote(ex.at[(x + s) % N_X, 1 - core], ex_near.at[s], s_xn.at[s], r_xn.at[s], sibling) for s in (2, 1, 3, 0)
    }

    piece = err_slab[z]
    for s in near_first:
        e_z[s].wait_recv()
        piece = piece + err_z[s]
    err_full[y, z] = piece * (1.0 / (N_Y * N_Z))
    here = err_full.at[y, z]
    e_zz = {s: remote(here, here, s_ezz.at[s], r_ezz.at[s], z_peer(s)) for s in z_steps}

    t_y = {}
    x_far = {}
    for c in (2, 1, 3, 0):
        rows = slab_rows((y + c) % N_Y)
        for s in (1, 3, 2):
            second[s, c].wait_recv()
        total = merged[rows, :] + far[1, rows].astype(F32) + far[3, rows].astype(F32) + far[2, rows].astype(F32)
        total = total * (1.0 / N_MP)
        merged[rows, :split] = total[:, :split] + in_error[rows, :]
        merged[rows, split:] = total[:, split:] + out_error[rows, :]
        if c:
            sum_src[rows, :] = total.astype(BF16)
            t_y[c] = remote(sum_src.at[rows], sum_y.at[c], s_ty.at[c], r_ty.at[c], y_peer(c))
        if c == 2:
            for s in four:
                x_near[s].wait_recv()
                ex_mine[s] = ex[(x + s) % N_X, core] + ex_near[s]
                x_far[s] = remote(ex_mine.at[s], ex_far.at[s], s_xf.at[s], r_xf.at[s], x_peer(s))
    for s in four:
        t_y[s].wait_recv()
        total = total + sum_y[s].astype(F32)
    for k in range(N_Z):
        sum_slab[k] = total[:, 128 * k : 128 * (k + 1)]
    rounded = sum_slab[...].astype(BF16)
    sum_send = sum_full.at[N_Y]
    sum_full[N_Y] = rounded
    t_z = {s: remote(sum_send.at[(z + s) % N_Z], sum_z.at[s], s_tz.at[s], r_tz.at[s], z_peer(s)) for s in z_steps}

    x_near[0].wait_recv()
    part = ex[x, core] + ex_near[0]
    for s in four:
        x_far[s].wait_recv()
        part = part + ex_far[s]
    ex_part[0] = part
    x_y = {s: remote(ex_part.at[0], ex_y.at[s], s_xy.at[s], r_xy.at[s], y_peer(s)) for s in four}

    for s in near_first:
        e_zz[s].wait_recv()
    here = err_full.at[y]
    e_yy = {s: remote(here, here, s_eyy.at[s], r_eyy.at[s], y_peer(s)) for s in four}

    piece = sum_slab[z]
    for s in near_first:
        t_z[s].wait_recv()
        piece = piece + sum_z[s].astype(F32)
    sum_full[y, z] = (piece * (1.0 / (N_Y * N_Z))).astype(BF16)
    here = sum_full.at[y, z]
    t_zz = {s: remote(here, here, s_tzz.at[s], r_tzz.at[s], z_peer(s)) for s in z_steps}

    for s in four:
        x_y[s].wait_recv()
        part = part + ex_y[s]
    ex_part[1] = part
    x_z = {s: remote(ex_part.at[1], ex_z.at[s], s_xz.at[s], r_xz.at[s], z_peer(s)) for s in z_steps}

    for s in near_first:
        t_zz[s].wait_recv()
    here = sum_full.at[y]
    t_yy = {s: remote(here, here, s_tyy.at[s], r_tyy.at[s], y_peer(s)) for s in four}

    for s in near_first:
        x_z[s].wait_recv()
        part = part + ex_z[s]
    extra_all[mp] = part
    here = extra_all.at[mp]
    x_x = {s: remote(here, here, s_xx.at[s], r_xx.at[s], x_peer(s)) for s in four}
    x_s = [remote(here, here, s_xs.at[0], r_xs.at[0], sibling)]

    def finish(slab):
        for k in range(N_Z):
            mean[slab_rows(slab), 128 * k : 128 * (k + 1)] = err_full[slab, k] + sum_full[slab, k].astype(F32)

    finish(y)
    for s in (1, 3, 2):
        x_x[s].wait_recv()
        here = extra_all.at[2 * ((x + N_X - s) % N_X) + core]
        x_s.append(remote(here, here, s_xs.at[s], r_xs.at[s], sibling))
    for s in (1, 3, 2):
        e_yy[s].wait_recv()
        t_yy[s].wait_recv()
        finish((y + N_Y - s) % N_Y)
    for copy in x_s:
        copy.wait_recv()
    for copy in sent:
        copy.wait_send()


def layer(*operands):
    def vmem(*shape, dtype=F32):
        return pltpu.VMEM(shape, dtype)

    def dma(*shape):
        return [pltpu.SemaphoreType.DMA(shape)] * 2

    return pl.pallas_call(
        layer_kernel,
        out_shape=(
            jax.ShapeDtypeStruct((ROWS, WIDTH), BF16),
            jax.ShapeDtypeStruct((BLOCK, COLS), F32),
            jax.ShapeDtypeStruct((BLOCK, COLS), F32),
            jax.ShapeDtypeStruct((N_MP, 8, 128), F32),
        ),
        in_specs=[HBM] * 7 + [VMEM] * 4,
        out_specs=(VMEM,) * 4,
        scratch_shapes=[pltpu.VMEM(a.shape, a.dtype) for a in operands[:7]]
        + [pltpu.SemaphoreType.DMA((7,))]
        + [
            vmem(ROWS, 3 * WIDTH, dtype=BF16),
            vmem(ROWS, WIDTH, dtype=BF16),
            vmem(ROWS, WIDTH, dtype=BF16),
            vmem(ROWS, 3 * WIDTH, dtype=BF16),
            vmem(ROWS, WIDTH),
            vmem(HEADS, SPAN, SPAN),
            vmem(HEADS, SPAN, SPAN),
            vmem(N_X, 2 * BLOCK, COLS, dtype=BF16),
            vmem(N_X, BLOCK, COLS, dtype=BF16),
            vmem(N_X, BLOCK, COLS, dtype=BF16),
            vmem(N_X, BLOCK, COLS, dtype=BF16),
            vmem(N_Y, 16, COLS),
            vmem(N_Z, 16, 128),
            vmem(N_Z, 16, 128),
            vmem(N_Y, N_Z, 16, 128),
            vmem(BLOCK, COLS, dtype=BF16),
            vmem(N_Y, 16, COLS, dtype=BF16),
            vmem(N_Z, 16, 128),
            vmem(N_Z, 16, 128, dtype=BF16),
            vmem(N_Y + 1, N_Z, 16, 128, dtype=BF16),
            vmem(N_X, 2, 8, 128),
            vmem(N_X, 8, 128),
            vmem(N_X, 8, 128),
            vmem(N_X, 8, 128),
            vmem(2, 8, 128),
            vmem(N_Y, 8, 128),
            vmem(N_Z, 8, 128),
        ]
        + dma(4) + dma(4, 4)
        + dma(4, 2) + dma(N_Z) + dma(N_Z) + dma(4)
        + dma(4) + dma(N_Z) + dma(N_Z) + dma(4)
        + dma(4) + dma(4) + dma(4) + dma(N_Z) + dma(4) + dma(4),
        compiler_params=pltpu.CompilerParams(collective_id=1, has_side_effects=True, vmem_limit_bytes=48 << 20),
        name="layer",
    )(*(pltpu.with_memory_space_constraint(a, pltpu.HBM) for a in operands[:7]), *operands[7:])


def orthonormal_rows(left):
    lane = lax.broadcasted_iota(jnp.int32, (8, 128), 1)
    row = lax.broadcasted_iota(jnp.int32, (8, 128), 0)
    is_in = lane < BLOCK
    zero = jnp.zeros((8, 128), F32)

    def lane_sum(a):
        return jnp.sum(a, axis=1, keepdims=True)

    columns = [left[8 * g : 8 * g + 8, :] for g in range(4)]
    in_columns = [jnp.where(is_in, v, 0.0) for v in columns]
    out_columns = [jnp.where(is_in, 0.0, v) for v in columns]
    taken = [zero] * 4
    in_w, out_w, in_wr, out_wr, squares = ([zero] * 4 for _ in range(5))
    for c in range(32):
        g, at = c // 8, c % 8
        here = row == at
        vector = jnp.broadcast_to((columns[g] - taken[g])[at : at + 1, :], (8, 128))
        if c:
            total = None
            for k in range(g + 1):
                term = in_wr[k] * lane_sum(in_w[k] * vector) + out_wr[k] * lane_sum(out_w[k] * vector)
                total = term if total is None else total + term
            vector = vector - jnp.sum(total, axis=0, keepdims=True)
        in_v, out_v = jnp.where(is_in, vector, 0.0), jnp.where(is_in, 0.0, vector)
        square = jnp.where(is_in, lane_sum(in_v * in_v), lane_sum(out_v * out_v))
        share = 1.0 / (square + BASIS_EPS)
        in_scaled, out_scaled = in_v * share, out_v * share
        for k in range(g, 4):
            taken[k] = (
                taken[k] + in_scaled * lane_sum(in_columns[k] * vector) + out_scaled * lane_sum(out_columns[k] * vector)
            )
        in_w[g], out_w[g] = jnp.where(here, in_v, in_w[g]), jnp.where(here, out_v, out_w[g])
        in_wr[g], out_wr[g] = jnp.where(here, in_scaled, in_wr[g]), jnp.where(here, out_scaled, out_wr[g])
        squares[g] = jnp.where(here, square, squares[g])
    return jnp.concatenate([(in_w[g] + out_w[g]) * lax.rsqrt(squares[g] + BASIS_EPS) for g in range(4)], axis=0)


def factor_kernel(
    mean, merged, in_basis, out_basis, extra, token_grad_in,
    in_update, out_update, in_error, out_error, in_right, out_right, gain_grad, table_grad, token_grad, left,
):
    split = 3 * WIDTH
    left[:, :BLOCK] = nt(in_basis[...], mean[:, :split], precision=HIGH)
    left[:, BLOCK:] = nt(out_basis[...], mean[:, split:], precision=HIGH)
    ortho = orthonormal_rows(left)
    in_ortho, out_ortho = ortho[:, :BLOCK], ortho[:, BLOCK:]
    right = nn(in_ortho, mean[:, :split], precision=HIGH)
    in_right[...] = right
    update = tn(in_ortho, right, precision=HIGH)
    in_update[...] = update
    in_error[...] = merged[:, :split] - update
    right = nn(out_ortho, mean[:, split:], precision=HIGH)
    out_right[...] = right
    update = tn(out_ortho, right, precision=HIGH)
    out_update[...] = update
    out_error[...] = merged[:, split:] - update

    share = 1.0 / (N_Y * N_Z * N_MP)
    buckets = table_grad.shape[1]
    for head in range(HEADS):
        for c in range(CHUNKS):
            width = min(128, buckets - 128 * c)
            table_grad[head : head + 1, 128 * c : 128 * c + width] = extra[head, c : c + 1, :width] * share
    for pair in range(HEADS // 2):
        low, high = extra[2 * pair, 6:7, :], pltpu.roll(extra[2 * pair + 1, 6:7, :], 64, 1)
        lane = lax.broadcasted_iota(jnp.int32, (1, 128), 1)
        gain_grad[:, 128 * pair : 128 * (pair + 1)] = jnp.where(lane < 64, low, high) * share
    token_grad[...] = token_grad_in[...]


def factors(buckets, *operands):
    wide = jax.ShapeDtypeStruct((BLOCK, 3 * WIDTH), F32)
    thin = jax.ShapeDtypeStruct((BLOCK, WIDTH), F32)
    return pl.pallas_call(
        factor_kernel,
        out_shape=(
            wide, thin, wide, thin,
            jax.ShapeDtypeStruct((32, 3 * WIDTH), F32),
            jax.ShapeDtypeStruct((32, WIDTH), F32),
            jax.ShapeDtypeStruct((1, WIDTH), F32),
            jax.ShapeDtypeStruct((HEADS, buckets), F32),
            jax.ShapeDtypeStruct((ROWS, WIDTH), BF16),
        ),
        in_specs=[VMEM] * len(operands),
        out_specs=(VMEM,) * 9,
        scratch_shapes=[pltpu.VMEM((32, 128), F32)],
        compiler_params=pltpu.CompilerParams(vmem_limit_bytes=32 << 20),
        name="factors",
    )(*operands)


def shards(
    tokens,
    cotangent,
    region_ids,
    rel_bucket,
    norm_gain,
    in_weight,
    out_weight,
    bias_table,
    in_error,
    out_error,
    in_basis,
    out_basis,
):
    tok = tokens.reshape(ROWS, WIDTH)
    gain = norm_gain.reshape(1, WIDTH)
    full_in, full_out, bias, normed = gather_weights(in_weight, out_weight, bias_table, rel_bucket, tok, gain)
    token_grad, merged, mean, extra_all = layer(
        cotangent.reshape(ROWS, WIDTH), region_ids, in_error[0], out_error[0], tok, gain, rel_bucket,
        bias, normed, full_in, full_out,
    )
    in_update, out_update, in_new, out_new, in_right, out_right, gain_grad, table_grad, token_grad = factors(
        bias_table.shape[1], mean, merged, in_basis[0].T, out_basis[0].T, extra_all, token_grad
    )
    return (
        token_grad.reshape(tokens.shape),
        gain_grad.reshape(WIDTH),
        table_grad,
        in_update,
        out_update,
        in_new[None],
        out_new[None],
        in_right.T[None],
        out_right.T[None],
    )


def solution(mesh):
    placed = (
        P(("dp", "mp"), None, None),
        P(("dp", "mp"), None, None),
        P(("dp", "mp"), None),
        P(),
        P(),
        P("mp", None),
        P("mp", None),
        P(),
        P("dp", "mp", None),
        P("dp", "mp", None),
        P("mp", None, None),
        P("mp", None, None),
    )
    return jax.shard_map(
        shards,
        mesh=mesh,
        in_specs=placed,
        out_specs=(
            P(("dp", "mp"), None, None),
            P(),
            P(),
            P("mp", None),
            P("mp", None),
            P("dp", "mp", None),
            P("dp", "mp", None),
            P("mp", None, None),
            P("mp", None, None),
        ),
        check_vma=False,
    )
```

```python
import jax
import jax.numpy as jnp
from jax import lax
from jax.experimental import pallas as pl
from jax.experimental.pallas import tpu as pltpu
from jax.sharding import PartitionSpec as P

NORM_EPS = 1e-05
BASIS_EPS = 1e-06
MASKED = -1e30
HIGH = lax.Precision.HIGHEST
MESH = pl.DeviceIdType.MESH
F32 = jnp.float32
BF16 = jnp.bfloat16
VMEM = pl.BlockSpec(memory_space=pltpu.VMEM)
HBM = pl.BlockSpec(memory_space=pltpu.HBM)

WIN, SPAN, WIDTH, HEADS, CHUNKS = 2, 144, 512, 8, 6
ROWS = WIN * SPAN
N_X, N_Y, N_Z, N_MP = 4, 4, 16, 8
BLOCK = 64
COLS = 4 * WIDTH


def nt(a, b, **kw):
    return lax.dot_general(a, b, (((1,), (1,)), ((), ())), preferred_element_type=F32, **kw)


def tn(a, b, **kw):
    return lax.dot_general(a, b, (((0,), (0,)), ((), ())), preferred_element_type=F32, **kw)


def nn(a, b, **kw):
    return jnp.dot(a, b, preferred_element_type=F32, **kw)


def gather_kernel(
    in_ref, out_ref, table_hbm, bucket_hbm, tok_hbm, gain_hbm,
    full_in, full_out, bias_ref, normed_ref, flipped_ref,
    table_ref, bucket_ref, tok_ref, gain_ref, index, table, send, recv, rsend, rrecv, fsend, frecv, local,
):
    mp = lax.axis_index("mp")
    x, core = mp // 2, mp % 2
    sibling = {"mp": 2 * x + 1 - core}

    def device(step):
        return 2 * ((x + step) % N_X) + core

    right, left = {"mp": device(1)}, {"mp": device(3)}
    barrier = pltpu.get_barrier_semaphore()
    for target in (right, left, sibling):
        pl.semaphore_signal(barrier, inc=1, device_id=target, device_id_type=MESH)

    sources, fulls = (in_ref, out_ref), (full_in, full_out)
    half_rows = BLOCK // 2

    def rows(owner):
        return pl.ds(pl.multiple_of(owner * BLOCK, BLOCK), BLOCK)

    def half(owner, h):
        return pl.ds(pl.multiple_of(owner * BLOCK + h * half_rows, half_rows), half_rows)

    own = [pltpu.make_async_copy(sources[k], fulls[k].at[rows(mp)], local.at[k]) for k in range(2)]
    staged = [
        pltpu.make_async_copy(src, dst, local.at[2 + k])
        for k, (src, dst) in enumerate(
            ((table_hbm, table_ref), (bucket_hbm, bucket_ref), (tok_hbm, tok_ref), (gain_hbm, gain_ref))
        )
    ]
    for copy in staged + own:
        copy.start()
    for copy in staged:
        copy.wait()
    index[...] = jnp.zeros_like(index)
    index[:, :SPAN] = bucket_ref[...]
    table[...] = jnp.zeros_like(table)
    table[:, : table_ref.shape[1]] = table_ref[...]
    pl.semaphore_wait(barrier, 3)

    started = []

    def remote(src, dst, send_sem, recv_sem, target):
        copy = pltpu.make_async_remote_copy(src, dst, send_sem, recv_sem, device_id=target, device_id_type=MESH)
        copy.start()
        started.append(copy)
        return copy

    first = {}
    for turn in range(2):
        for k in range(2):
            for way, target in ((0, right), (1, left)):
                h = turn ^ way
                first[way, k, h] = remote(
                    sources[k].at[pl.ds(h * half_rows, half_rows)], fulls[k].at[half(mp, h)],
                    send.at[way, k, h], recv.at[way, k, h], target,
                )
    passed = [
        remote(sources[k], fulls[k].at[rows(mp)], fsend.at[0, k, 0], frecv.at[0, k, 0], sibling) for k in range(2)
    ]

    def look_up(part):
        lanes = 128 if part == 0 else SPAN - 128

        @pl.loop(0, SPAN // 16)
        def _(block):
            at = pl.ds(pl.multiple_of(block * 16, 16), 16)
            bucket = index[at, pl.ds(part * 128, 128)]
            low = bucket & 127
            chunk = bucket >> 7
            for head in range(HEADS):
                found = jnp.zeros((16, 128), F32)
                for c in range(CHUNKS):
                    row = jnp.broadcast_to(table[head : head + 1, c * 128 : (c + 1) * 128], (16, 128))
                    found = jnp.where(chunk == c, jnp.take_along_axis(row, low, axis=1), found)
                bias_ref[head, at, part * 128 : part * 128 + lanes] = found[:, :lanes]

    def to_sibling(group, k, h, owner):
        slab = fulls[k].at[half(owner, h)]
        passed.append(remote(slab, slab, fsend.at[group, k, h], frecv.at[group, k, h], sibling))

    look_up(0)
    relayed = {}
    for k in range(2):
        for way, target in ((0, right), (1, left)):
            h = way
            first[way, k, h].wait_recv()
            owner = device(3 if way == 0 else 1)
            slab = fulls[k].at[half(owner, h)]
            relayed[way, k] = remote(slab, slab, rsend.at[way, k], rrecv.at[way, k], target)
            to_sibling(1 + way, k, h, owner)
    look_up(1)
    wide = tok_ref[...].astype(F32)
    centered = wide - jnp.mean(wide, axis=-1, keepdims=True)
    inv_sigma = lax.rsqrt(jnp.mean(centered * centered, axis=-1, keepdims=True) + NORM_EPS)
    rounded = (centered * inv_sigma * gain_ref[...]).astype(BF16)
    normed_ref[...] = rounded
    flipped_ref[...] = rounded.T
    for k in range(2):
        for way in range(2):
            first[way, k, 1 - way].wait_recv()
            to_sibling(1 + way, k, 1 - way, device(3 if way == 0 else 1))
    for k in range(2):
        for way in range(2):
            relayed[way, k].wait_recv()
            to_sibling(3, k, way, device(2))
    for copy in own:
        copy.wait()
    for copy in passed:
        copy.wait_recv()
    for copy in started:
        copy.wait_send()


def gather_weights(*operands):
    def dma(*shape):
        return [pltpu.SemaphoreType.DMA(shape)] * 2

    return pl.pallas_call(
        gather_kernel,
        out_shape=(
            jax.ShapeDtypeStruct((WIDTH, 3 * WIDTH), BF16),
            jax.ShapeDtypeStruct((WIDTH, WIDTH), BF16),
            jax.ShapeDtypeStruct((HEADS, SPAN, SPAN), F32),
            jax.ShapeDtypeStruct((ROWS, WIDTH), BF16),
            jax.ShapeDtypeStruct((WIDTH, ROWS), BF16),
        ),
        in_specs=[HBM] * len(operands),
        out_specs=(VMEM,) * 5,
        scratch_shapes=[pltpu.VMEM(a.shape, a.dtype) for a in operands[2:]]
        + [pltpu.VMEM((SPAN, 256), jnp.int32), pltpu.VMEM((HEADS, CHUNKS * 128), F32)]
        + dma(2, 2, 2) + dma(2, 2) + dma(4, 2, 2)
        + [pltpu.SemaphoreType.DMA((6,))],
        compiler_params=pltpu.CompilerParams(collective_id=0, has_side_effects=True, vmem_limit_bytes=32 << 20),
        name="gather_weights",
    )(*(pltpu.with_memory_space_constraint(a, pltpu.HBM) for a in operands))


def orthonormal_rows(left, halfway):
    lane = lax.broadcasted_iota(jnp.int32, (8, 128), 1)
    row = lax.broadcasted_iota(jnp.int32, (8, 128), 0)
    is_in = lane < BLOCK
    zero = jnp.zeros((8, 128), F32)

    def lane_sum(a):
        return jnp.sum(a, axis=1, keepdims=True)

    columns = [left[8 * g : 8 * g + 8, :] for g in range(4)]
    in_columns = [jnp.where(is_in, v, 0.0) for v in columns]
    out_columns = [jnp.where(is_in, 0.0, v) for v in columns]
    taken = [zero] * 4
    in_w, out_w, in_wr, out_wr, squares = ([zero] * 4 for _ in range(5))
    for c in range(32):
        g, at = c // 8, c % 8
        if c == 16:
            halfway()
        here = row == at
        vector = jnp.broadcast_to((columns[g] - taken[g])[at : at + 1, :], (8, 128))
        if c:
            total = None
            for k in range(g + 1):
                term = in_wr[k] * lane_sum(in_w[k] * vector) + out_wr[k] * lane_sum(out_w[k] * vector)
                total = term if total is None else total + term
            vector = vector - jnp.sum(total, axis=0, keepdims=True)
        in_v, out_v = jnp.where(is_in, vector, 0.0), jnp.where(is_in, 0.0, vector)
        square = jnp.where(is_in, lane_sum(in_v * in_v), lane_sum(out_v * out_v))
        share = 1.0 / (square + BASIS_EPS)
        in_scaled, out_scaled = in_v * share, out_v * share
        for k in range(g, 4):
            taken[k] = (
                taken[k] + in_scaled * lane_sum(in_columns[k] * vector) + out_scaled * lane_sum(out_columns[k] * vector)
            )
        in_w[g], out_w[g] = jnp.where(here, in_v, in_w[g]), jnp.where(here, out_v, out_w[g])
        in_wr[g], out_wr[g] = jnp.where(here, in_scaled, in_wr[g]), jnp.where(here, out_scaled, out_wr[g])
        squares[g] = jnp.where(here, square, squares[g])
    return jnp.concatenate([(in_w[g] + out_w[g]) * lax.rsqrt(squares[g] + BASIS_EPS) for g in range(4)], axis=0)


def layer_kernel(
    cot_hbm, region_hbm, in_error_hbm, out_error_hbm, tok_hbm, gain_hbm, bucket_hbm, in_basis_hbm, out_basis_hbm,
    bias_ref, normed, flipped, win_ref, wout_ref,
    tokgrad_ref, merged, mean, extra_all, ortho,
    cot_ref, region_ref, in_error, out_error, tok_ref, gain_ref, bucket_ref, in_basis, out_basis, staging,
    proj, mixgrad, mixed, packed, x_hat, score_high, score_low,
    prod, near, mine, far, out_prod, out_near, out_mine, out_far,
    err_y, err_slab, err_z, err_full,
    sum_src, out_src, sum_own, sum_y, sum_slab, sum_z, sum_full,
    ex, ex_near, ex_mine, ex_far, ex_part, ex_y, ex_z, left_all,
    s_near, r_near, s_far, r_far, s_fo, r_fo,
    s_ey, r_ey, s_ez, r_ez, s_ezz, r_ezz, s_eyy, r_eyy,
    s_ty, r_ty, s_tz, r_tz, s_tzz, r_tzz, s_tyy, r_tyy,
    s_xn, r_xn, s_xf, r_xf, s_xy, r_xy, s_xz, r_xz, s_xx, r_xx, s_xs, r_xs, s_l, r_l,
):
    dp, mp = lax.axis_index("dp"), lax.axis_index("mp")
    z, y, x, core = dp // N_Y, dp % N_Y, mp // 2, mp % 2
    sibling = {"mp": 2 * x + 1 - core}
    split = 3 * WIDTH

    def x_peer(step):
        return {"mp": 2 * ((x + step) % N_X) + core}

    def y_peer(step):
        return {"dp": z * N_Y + (y + step) % N_Y}

    def z_peer(step):
        return {"dp": ((z + step) % N_Z) * N_Y + y}

    sent = []

    def remote(src, dst, send, recv, target):
        copy = pltpu.make_async_remote_copy(src, dst, send, recv, device_id=target, device_id_type=MESH)
        copy.start()
        sent.append(copy)
        return copy

    def slab_rows(index):
        return pl.ds(pl.multiple_of(index * 16, 16), 16)

    four = (2, 1, 3)
    z_steps = (8, 7, 9, 6, 10, 5, 11, 4, 12, 3, 13, 2, 14, 1, 15)
    near_first = tuple(reversed(z_steps))

    barrier = pltpu.get_barrier_semaphore()
    peers = [z_peer(s) for s in z_steps] + [y_peer(s) for s in four] + [x_peer(s) for s in four] + [sibling]
    for target in peers:
        pl.semaphore_signal(barrier, inc=1, device_id=target, device_id_type=MESH)

    staged = [
        pltpu.make_async_copy(src, dst, staging.at[k])
        for k, (src, dst) in enumerate(
            (
                (cot_hbm, cot_ref), (region_hbm, region_ref), (in_error_hbm, in_error), (out_error_hbm, out_error),
                (tok_hbm, tok_ref), (gain_hbm, gain_ref), (bucket_hbm, bucket_ref),
                (in_basis_hbm, in_basis), (out_basis_hbm, out_basis),
            )
        )
    ]
    for copy in staged:
        copy.start()

    proj[...] = nn(normed[...], win_ref[...]).astype(BF16)
    for copy in staged:
        copy.wait()
    mixgrad[...] = nt(cot_ref[...], wout_ref[...]).astype(BF16)

    lane = lax.broadcasted_iota(jnp.int32, (1, 128), 1)
    first_half = lane < 64
    halves = (first_half.astype(BF16), (lane >= 64).astype(BF16))
    scale = jnp.asarray(0.125, BF16)
    allowed = []
    for w in range(WIN):
        square = jnp.broadcast_to(region_ref[w : w + 1, :].astype(F32), (SPAN, SPAN))
        allowed.append(square == square.T)

    def heads(pair):
        at = [pl.ds(pl.multiple_of(k * WIDTH + pair * 128, 128), 128) for k in range(3)]
        grads = [[], []]
        for w in range(WIN):
            rows = pl.ds(w * SPAN, SPAN)
            q = proj[rows, at[0]] * scale
            key = proj[rows, at[1]]
            value = proj[rows, at[2]]
            key_scaled = key * scale
            grad = mixgrad[rows, at[0]]
            parts = []
            for t in range(2):
                scores = nt(q * halves[t], key) + bias_ref[2 * pair + t]
                scores = jnp.where(allowed[w], scores, MASKED)
                exps = jnp.exp(scores - jnp.max(scores, axis=-1, keepdims=True))
                prob = exps * (1.0 / jnp.sum(exps, axis=-1, keepdims=True))
                prob_b = prob.astype(BF16)
                out = nn(prob_b, value)
                prob_grad = nt(grad * halves[t], value)
                value_grad = tn(prob_b, grad)
                score_grad = prob * (prob_grad - jnp.sum(prob * prob_grad, axis=-1, keepdims=True))
                grads[t].append(score_grad)
                score_b = score_grad.astype(BF16)
                parts.append((nn(score_b, key_scaled), tn(score_b, q), value_grad, out))
            joined = [jnp.where(first_half, a, b).astype(BF16) for a, b in zip(*parts)]
            for k in range(3):
                packed[rows, at[k]] = joined[k]
            mixed[rows, :] = joined[3]
        for t in range(2):
            total = grads[t][0] + grads[t][1]
            high = total.astype(BF16).astype(F32)
            score_high[2 * pair + t] = high
            score_low[2 * pair + t] = total - high
        return at

    order = (2, 1, 3, 0)
    near_in, near_out, far_in, far_out = {}, {}, {}, {}

    def send_near(i, at):
        columns = jnp.concatenate([packed[:, at[k]] for k in range(3)], axis=1)
        terms = nn(flipped[...], columns).astype(BF16)
        for m in range(N_MP):
            prod[i, m // 2, m % 2] = terms[m * BLOCK : (m + 1) * BLOCK]
        out_terms = tn(mixed[...], cot_ref[...]).astype(BF16)
        for c in range(2):
            out_prod[i, c] = out_terms[c * BLOCK : (c + 1) * BLOCK]
        near_in[i] = remote(prod.at[i, :, 1 - core], near.at[i], s_near.at[i, 0], r_near.at[i, 0], sibling)
        near_out[i] = remote(out_prod.at[i, 1 - core], out_near.at[i], s_near.at[i, 1], r_near.at[i, 1], sibling)

    def send_far(i):
        near_in[i].wait_recv()
        for s in four:
            chip = (x + s) % N_X
            mine[i, s] = (prod[i, chip, core].astype(F32) + near[i, chip].astype(F32)).astype(BF16)
            pair = pair_of(i)
            far_in[i, s] = remote(mine.at[i, s], far.at[pair, s], s_far.at[i, s], r_far.at[pair, s], x_peer(s))
        near_out[i].wait_recv()
        s = order[i]
        if s:
            out_mine[s] = (out_prod[i, core].astype(F32) + out_near[i].astype(F32)).astype(BF16)
            far_out[s] = remote(out_mine.at[s], out_far.at[s], s_fo.at[s], r_fo.at[s], x_peer(s))

    def pair_of(i):
        return (x + order[i]) % N_X

    e_y = []

    def error_over_y():
        for s in four:
            rows = slab_rows((y + s) % N_Y)
            e_y.append(remote(in_error.at[rows], err_y.at[s, :, pl.ds(0, split)], s_ey.at[s, 0], r_ey.at[s, 0], y_peer(s)))
            e_y.append(
                remote(out_error.at[rows], err_y.at[s, :, pl.ds(split, WIDTH)], s_ey.at[s, 1], r_ey.at[s, 1], y_peer(s))
            )

    for i in range(4):
        at = heads(pair_of(i))
        if i == 0:
            pl.semaphore_wait(barrier, len(peers))
        send_near(i, at)
        if i == 0:
            error_over_y()
        if i:
            send_far(i - 1)


    for copy in e_y:
        copy.wait_recv()
    err = err_y[1] + err_y[2] + err_y[3]
    err_in = err[:, :split] + in_error[slab_rows(y), :]
    err_out = err[:, split:] + out_error[slab_rows(y), :]
    for k in range(N_Z):
        src = err_in if k < 12 else err_out
        err_slab[k] = src[:, 128 * (k % 12) : 128 * (k % 12) + 128]
    e_z = {s: remote(err_slab.at[(z + s) % N_Z], err_z.at[s], s_ez.at[s], r_ez.at[s], z_peer(s)) for s in z_steps}

    gain = gain_ref[...]
    wide = tok_ref[...].astype(F32)
    centered = wide - jnp.mean(wide, axis=-1, keepdims=True)
    inv_sigma = lax.rsqrt(jnp.mean(centered * centered, axis=-1, keepdims=True) + NORM_EPS)
    x_hat[...] = centered * inv_sigma
    normed_grad = nt(packed[...], win_ref[...])
    gain_term = jnp.sum(normed_grad * x_hat[...], axis=0, keepdims=True)
    hat_grad = normed_grad * gain
    delta = inv_sigma * (
        hat_grad
        - jnp.mean(hat_grad, axis=-1, keepdims=True)
        - x_hat[...] * jnp.mean(hat_grad * x_hat[...], axis=-1, keepdims=True)
    )
    tokgrad_ref[...] = (cot_ref[...].astype(F32) + delta).astype(BF16)

    send_far(3)

    chunk_row = lax.broadcasted_iota(jnp.int32, (8, SPAN), 0)
    within = lax.broadcasted_iota(jnp.int32, (128, SPAN), 0)

    def add_rows(block, total):
        for k in range(16):
            i = block * 16 + k
            bucket = bucket_ref[pl.ds(i, 1), :]
            chunk_is = jnp.broadcast_to(bucket >> 7, (8, SPAN)) == chunk_row
            one_hot = jnp.where(jnp.broadcast_to(bucket & 127, (128, SPAN)) == within, 1.0, 0.0).astype(BF16)
            picked = jnp.concatenate(
                [
                    jnp.where(chunk_is, jnp.broadcast_to(part[head, pl.ds(i, 1), :], (8, SPAN)), 0.0)
                    for part in (score_high, score_low)
                    for head in range(HEADS)
                ],
                axis=0,
            ).astype(BF16)
            total = total + nt(picked, one_hot)
        return total

    total = lax.fori_loop(0, SPAN // 16, add_rows, jnp.zeros((128, 128), F32))
    table_term = total[:64] + total[64:]
    for head in range(HEADS):
        ex[head // 2, head % 2] = table_term[8 * head : 8 * head + 8]
        part = gain_term[:, 128 * (head // 2) : 128 * (head // 2 + 1)]
        if head % 2:
            part = pltpu.roll(part, 64, 1)
        ex[head // 2, head % 2, 6:7, :] = part
    x_near = {
        s: remote(ex.at[(x + s) % N_X, 1 - core], ex_near.at[s], s_xn.at[s], r_xn.at[s], sibling) for s in (2, 1, 3, 0)
    }

    t_y = {}
    totals = []

    def send_y(j, total, src, width):
        src[...] = total.astype(BF16)
        for s in four:
            rows = slab_rows((y + s) % N_Y)
            t_y[j, s] = remote(
                src.at[rows], sum_y.at[j, s, :, pl.ds(0, width)], s_ty.at[j, s], r_ty.at[j, s], y_peer(s)
            )

    for i in range(4):
        total = prod[i, x, core].astype(F32) + near[i, x].astype(F32)
        for s in (1, 3, 2):
            far_in[i, s].wait_recv()
            total = total + far[pair_of(i), s].astype(F32)
        total = total * (1.0 / N_MP)
        for k in range(3):
            cols = pl.ds(pl.multiple_of(k * WIDTH + pair_of(i) * 128, 128), 128)
            merged[:, cols] = total[:, 128 * k : 128 * (k + 1)] + in_error[:, cols]
        send_y(i, total, sum_src.at[i], 384)
        sum_own[i, :, :384] = total
    total = out_prod[3, core].astype(F32) + out_near[3].astype(F32)
    for s in (2, 1, 3):
        far_out[s].wait_recv()
        total = total + out_far[s].astype(F32)
    total = total * (1.0 / N_MP)
    merged[:, split:] = total + out_error[...]
    send_y(4, total, out_src, WIDTH)
    sum_own[4] = total

    piece = err_slab[z]
    for s in near_first:
        e_z[s].wait_recv()
        piece = piece + err_z[s]
    err_full[y, z] = piece * (1.0 / (N_Y * N_Z))
    here = err_full.at[y, z]
    e_zz = {s: remote(here, here, s_ezz.at[s], r_ezz.at[s], z_peer(s)) for s in z_steps}

    x_far = {}
    for s in four:
        x_near[s].wait_recv()
        ex_mine[s] = ex[(x + s) % N_X, core] + ex_near[s]
        x_far[s] = remote(ex_mine.at[s], ex_far.at[s], s_xf.at[s], r_xf.at[s], x_peer(s))

    for j in range(5):
        total = sum_own[j, slab_rows(y), :]
        for s in (1, 3, 2):
            t_y[j, s].wait_recv()
            total = total + sum_y[j, s].astype(F32)
        for k in range(3 if j < 4 else 4):
            piece_at = 4 * k + pair_of(j) if j < 4 else 12 + k
            sum_slab[piece_at] = total[:, 128 * k : 128 * (k + 1)]
    rounded = sum_slab[...].astype(BF16)
    sum_send = sum_full.at[N_Y]
    sum_full[N_Y] = rounded
    t_z = {s: remote(sum_send.at[(z + s) % N_Z], sum_z.at[s], s_tz.at[s], r_tz.at[s], z_peer(s)) for s in z_steps}

    x_near[0].wait_recv()
    part = ex[x, core] + ex_near[0]
    for s in four:
        x_far[s].wait_recv()
        part = part + ex_far[s]
    ex_part[0] = part
    x_y = {s: remote(ex_part.at[0], ex_y.at[s], s_xy.at[s], r_xy.at[s], y_peer(s)) for s in four}

    piece = sum_slab[z]
    for s in near_first:
        t_z[s].wait_recv()
        piece = piece + sum_z[s].astype(F32)
    sum_full[y, z] = (piece * (1.0 / (N_Y * N_Z))).astype(BF16)
    here = sum_full.at[y, z]
    t_zz = {s: remote(here, here, s_tzz.at[s], r_tzz.at[s], z_peer(s)) for s in z_steps}

    for s in near_first:
        e_zz[s].wait_recv()
    here = err_full.at[y]
    e_yy = {s: remote(here, here, s_eyy.at[s], r_eyy.at[s], y_peer(s)) for s in four}

    for s in four:
        x_y[s].wait_recv()
        part = part + ex_y[s]
    ex_part[1] = part
    x_z = {s: remote(ex_part.at[1], ex_z.at[s], s_xz.at[s], r_xz.at[s], z_peer(s)) for s in z_steps}

    def finish(slab):
        for k in range(N_Z):
            mean[slab_rows(slab), 128 * k : 128 * (k + 1)] = err_full[slab, k] + sum_full[slab, k].astype(F32)

    for s in near_first:
        t_zz[s].wait_recv()
    finish(y)

    slab = mean[slab_rows(y), :]
    in_left = nt(slab[:, :split], in_basis[...], precision=HIGH)
    out_left = nt(slab[:, split:], out_basis[...], precision=HIGH)
    left_all[y] = jnp.concatenate([in_left, out_left, jnp.zeros((16, 64), F32)], axis=1)
    here = left_all.at[y]
    left_y = {s: remote(here, here, s_l.at[s], r_l.at[s], y_peer(s)) for s in four}
    here = sum_full.at[y]
    t_yy = {s: remote(here, here, s_tyy.at[s], r_tyy.at[s], y_peer(s)) for s in four}

    for s in near_first:
        x_z[s].wait_recv()
        part = part + ex_z[s]
    extra_all[mp] = part
    here = extra_all.at[mp]
    x_x = {s: remote(here, here, s_xx.at[s], r_xx.at[s], x_peer(s)) for s in four}
    x_s = [remote(here, here, s_xs.at[0], r_xs.at[0], sibling)]

    for s in (1, 3, 2):
        left_y[s].wait_recv()
    flipped_left = left_all[...].reshape(BLOCK, 128).T

    def halfway():
        for s in (1, 3, 2):
            x_x[s].wait_recv()
            here = extra_all.at[2 * ((x + N_X - s) % N_X) + core]
            x_s.append(remote(here, here, s_xs.at[s], r_xs.at[s], sibling))

    ortho[...] = orthonormal_rows(jnp.concatenate([flipped_left[:32], flipped_left[32:64]], axis=1), halfway)

    for s in (1, 3, 2):
        e_yy[s].wait_recv()
        t_yy[s].wait_recv()
        finish((y + N_Y - s) % N_Y)
    for copy in x_s:
        copy.wait_recv()
    for copy in sent:
        copy.wait_send()


def layer(*operands):
    def vmem(*shape, dtype=F32):
        return pltpu.VMEM(shape, dtype)

    def dma(*shape):
        return [pltpu.SemaphoreType.DMA(shape)] * 2

    return pl.pallas_call(
        layer_kernel,
        out_shape=(
            jax.ShapeDtypeStruct((ROWS, WIDTH), BF16),
            jax.ShapeDtypeStruct((BLOCK, COLS), F32),
            jax.ShapeDtypeStruct((BLOCK, COLS), F32),
            jax.ShapeDtypeStruct((N_MP, 8, 128), F32),
            jax.ShapeDtypeStruct((32, 2 * BLOCK), F32),
        ),
        in_specs=[HBM] * 9 + [VMEM] * 5,
        out_specs=(VMEM,) * 5,
        scratch_shapes=[pltpu.VMEM(a.shape, a.dtype) for a in operands[:9]]
        + [pltpu.SemaphoreType.DMA((9,))]
        + [
            vmem(ROWS, 3 * WIDTH, dtype=BF16),
            vmem(ROWS, WIDTH, dtype=BF16),
            vmem(ROWS, 128, dtype=BF16),
            vmem(ROWS, 3 * WIDTH, dtype=BF16),
            vmem(ROWS, WIDTH),
            vmem(HEADS, SPAN, SPAN),
            vmem(HEADS, SPAN, SPAN),
            vmem(4, N_X, 2, BLOCK, 384, dtype=BF16),
            vmem(4, N_X, BLOCK, 384, dtype=BF16),
            vmem(4, N_X, BLOCK, 384, dtype=BF16),
            vmem(4, N_X, BLOCK, 384, dtype=BF16),
            vmem(4, 2, BLOCK, WIDTH, dtype=BF16),
            vmem(4, BLOCK, WIDTH, dtype=BF16),
            vmem(N_X, BLOCK, WIDTH, dtype=BF16),
            vmem(N_X, BLOCK, WIDTH, dtype=BF16),
            vmem(N_Y, 16, COLS),
            vmem(N_Z, 16, 128),
            vmem(N_Z, 16, 128),
            vmem(N_Y, N_Z, 16, 128),
            vmem(4, BLOCK, 384, dtype=BF16),
            vmem(BLOCK, WIDTH, dtype=BF16),
            vmem(5, BLOCK, WIDTH),
            vmem(5, N_Y, 16, WIDTH, dtype=BF16),
            vmem(N_Z, 16, 128),
            vmem(N_Z, 16, 128, dtype=BF16),
            vmem(N_Y + 1, N_Z, 16, 128, dtype=BF16),
            vmem(N_X, 2, 8, 128),
            vmem(N_X, 8, 128),
            vmem(N_X, 8, 128),
            vmem(N_X, 8, 128),
            vmem(2, 8, 128),
            vmem(N_Y, 8, 128),
            vmem(N_Z, 8, 128),
            vmem(N_Y, 16, 128),
        ]
        + dma(4, 2) + dma(4, 4) + dma(4)
        + dma(4, 2) + dma(N_Z) + dma(N_Z) + dma(4)
        + dma(5, 4) + dma(N_Z) + dma(N_Z) + dma(4)
        + dma(4) + dma(4) + dma(4) + dma(N_Z) + dma(4) + dma(4) + dma(4),
        compiler_params=pltpu.CompilerParams(collective_id=1, has_side_effects=True, vmem_limit_bytes=48 << 20),
        name="layer",
    )(*(pltpu.with_memory_space_constraint(a, pltpu.HBM) for a in operands[:9]), *operands[9:])


def factor_kernel(
    mean, merged, ortho, extra, token_grad_in,
    in_update, out_update, in_error, out_error, in_right, out_right, gain_grad, table_grad, token_grad,
):
    split = 3 * WIDTH
    in_ortho, out_ortho = ortho[:, :BLOCK], ortho[:, BLOCK:]
    right = nn(in_ortho, mean[:, :split], precision=HIGH)
    in_right[...] = right
    update = tn(in_ortho, right, precision=HIGH)
    in_update[...] = update
    in_error[...] = merged[:, :split] - update
    right = nn(out_ortho, mean[:, split:], precision=HIGH)
    out_right[...] = right
    update = tn(out_ortho, right, precision=HIGH)
    out_update[...] = update
    out_error[...] = merged[:, split:] - update

    share = 1.0 / (N_Y * N_Z * N_MP)
    buckets = table_grad.shape[1]
    for head in range(HEADS):
        for c in range(CHUNKS):
            width = min(128, buckets - 128 * c)
            table_grad[head : head + 1, 128 * c : 128 * c + width] = extra[head, c : c + 1, :width] * share
    for pair in range(HEADS // 2):
        low, high = extra[2 * pair, 6:7, :], pltpu.roll(extra[2 * pair + 1, 6:7, :], 64, 1)
        lane = lax.broadcasted_iota(jnp.int32, (1, 128), 1)
        gain_grad[:, 128 * pair : 128 * (pair + 1)] = jnp.where(lane < 64, low, high) * share
    token_grad[...] = token_grad_in[...]


def factors(buckets, *operands):
    wide = jax.ShapeDtypeStruct((BLOCK, 3 * WIDTH), F32)
    thin = jax.ShapeDtypeStruct((BLOCK, WIDTH), F32)
    return pl.pallas_call(
        factor_kernel,
        out_shape=(
            wide, thin, wide, thin,
            jax.ShapeDtypeStruct((32, 3 * WIDTH), F32),
            jax.ShapeDtypeStruct((32, WIDTH), F32),
            jax.ShapeDtypeStruct((1, WIDTH), F32),
            jax.ShapeDtypeStruct((HEADS, buckets), F32),
            jax.ShapeDtypeStruct((ROWS, WIDTH), BF16),
        ),
        in_specs=[VMEM] * len(operands),
        out_specs=(VMEM,) * 9,
        compiler_params=pltpu.CompilerParams(vmem_limit_bytes=32 << 20),
        name="factors",
    )(*operands)


def shards(
    tokens,
    cotangent,
    region_ids,
    rel_bucket,
    norm_gain,
    in_weight,
    out_weight,
    bias_table,
    in_error,
    out_error,
    in_basis,
    out_basis,
):
    tok = tokens.reshape(ROWS, WIDTH)
    gain = norm_gain.reshape(1, WIDTH)
    full_in, full_out, bias, normed, flipped = gather_weights(in_weight, out_weight, bias_table, rel_bucket, tok, gain)
    token_grad, merged, mean, extra_all, ortho = layer(
        cotangent.reshape(ROWS, WIDTH), region_ids, in_error[0], out_error[0], tok, gain, rel_bucket,
        in_basis[0].T, out_basis[0].T,
        bias, normed, flipped, full_in, full_out,
    )
    in_update, out_update, in_new, out_new, in_right, out_right, gain_grad, table_grad, token_grad = factors(
        bias_table.shape[1], mean, merged, ortho, extra_all, token_grad
    )
    return (
        token_grad.reshape(tokens.shape),
        gain_grad.reshape(WIDTH),
        table_grad,
        in_update,
        out_update,
        in_new[None],
        out_new[None],
        in_right.T[None],
        out_right.T[None],
    )


def solution(mesh):
    placed = (
        P(("dp", "mp"), None, None),
        P(("dp", "mp"), None, None),
        P(("dp", "mp"), None),
        P(),
        P(),
        P("mp", None),
        P("mp", None),
        P(),
        P("dp", "mp", None),
        P("dp", "mp", None),
        P("mp", None, None),
        P("mp", None, None),
    )
    return jax.shard_map(
        shards,
        mesh=mesh,
        in_specs=placed,
        out_specs=(
            P(("dp", "mp"), None, None),
            P(),
            P(),
            P("mp", None),
            P("mp", None),
            P("dp", "mp", None),
            P("dp", "mp", None),
            P("mp", None, None),
            P("mp", None, None),
        ),
        check_vma=False,
    )
```

```python
import jax
import jax.numpy as jnp
from jax import lax
from jax.experimental import pallas as pl
from jax.experimental.pallas import tpu as pltpu
from jax.sharding import PartitionSpec as P

NORM_EPS = 1e-05
BASIS_EPS = 1e-06
MASKED = -1e30
HIGH = lax.Precision.HIGHEST
MESH = pl.DeviceIdType.MESH
F32 = jnp.float32
BF16 = jnp.bfloat16
VMEM = pl.BlockSpec(memory_space=pltpu.VMEM)
HBM = pl.BlockSpec(memory_space=pltpu.HBM)

WIN, SPAN, WIDTH, HEADS, CHUNKS = 2, 144, 512, 8, 6
ROWS = WIN * SPAN
N_X, N_Y, N_Z, N_MP = 4, 4, 16, 8
BLOCK = 64
COLS = 4 * WIDTH


def nt(a, b, **kw):
    return lax.dot_general(a, b, (((1,), (1,)), ((), ())), preferred_element_type=F32, **kw)


def tn(a, b, **kw):
    return lax.dot_general(a, b, (((0,), (0,)), ((), ())), preferred_element_type=F32, **kw)


def nn(a, b, **kw):
    return jnp.dot(a, b, preferred_element_type=F32, **kw)


def gather_kernel(
    in_ref, out_ref, table_hbm, bucket_hbm, tok_hbm, gain_hbm,
    full_in, full_out, bias_ref, normed_ref, flipped_ref,
    table_ref, bucket_ref, tok_ref, gain_ref, index, table, send, recv, rsend, rrecv, fsend, frecv, local,
):
    mp = lax.axis_index("mp")
    x, core = mp // 2, mp % 2
    sibling = {"mp": 2 * x + 1 - core}

    def device(step):
        return 2 * ((x + step) % N_X) + core

    right, left = {"mp": device(1)}, {"mp": device(3)}
    barrier = pltpu.get_barrier_semaphore()
    for target in (right, left, sibling):
        pl.semaphore_signal(barrier, inc=1, device_id=target, device_id_type=MESH)

    sources, fulls = (in_ref, out_ref), (full_in, full_out)
    half_rows = BLOCK // 2

    def rows(owner):
        return pl.ds(pl.multiple_of(owner * BLOCK, BLOCK), BLOCK)

    def half(owner, h):
        return pl.ds(pl.multiple_of(owner * BLOCK + h * half_rows, half_rows), half_rows)

    own = [pltpu.make_async_copy(sources[k], fulls[k].at[rows(mp)], local.at[k]) for k in range(2)]
    staged = [
        pltpu.make_async_copy(src, dst, local.at[2 + k])
        for k, (src, dst) in enumerate(
            ((table_hbm, table_ref), (bucket_hbm, bucket_ref), (tok_hbm, tok_ref), (gain_hbm, gain_ref))
        )
    ]
    for copy in staged + own:
        copy.start()
    for copy in staged:
        copy.wait()
    index[...] = jnp.zeros_like(index)
    index[:, :SPAN] = bucket_ref[...]
    table[...] = jnp.zeros_like(table)
    table[:, : table_ref.shape[1]] = table_ref[...]
    pl.semaphore_wait(barrier, 3)

    started = []

    def remote(src, dst, send_sem, recv_sem, target):
        copy = pltpu.make_async_remote_copy(src, dst, send_sem, recv_sem, device_id=target, device_id_type=MESH)
        copy.start()
        started.append(copy)
        return copy

    first = {}
    for turn in range(2):
        for k in range(2):
            for way, target in ((0, right), (1, left)):
                h = turn ^ way
                first[way, k, h] = remote(
                    sources[k].at[pl.ds(h * half_rows, half_rows)], fulls[k].at[half(mp, h)],
                    send.at[way, k, h], recv.at[way, k, h], target,
                )
    passed = [
        remote(sources[k], fulls[k].at[rows(mp)], fsend.at[0, k, 0], frecv.at[0, k, 0], sibling) for k in range(2)
    ]

    def look_up(part):
        lanes = 128 if part == 0 else SPAN - 128

        @pl.loop(0, SPAN // 16)
        def _(block):
            at = pl.ds(pl.multiple_of(block * 16, 16), 16)
            bucket = index[at, pl.ds(part * 128, 128)]
            low = bucket & 127
            chunk = bucket >> 7
            for head in range(HEADS):
                found = jnp.zeros((16, 128), F32)
                for c in range(CHUNKS):
                    row = jnp.broadcast_to(table[head : head + 1, c * 128 : (c + 1) * 128], (16, 128))
                    found = jnp.where(chunk == c, jnp.take_along_axis(row, low, axis=1), found)
                bias_ref[head, at, part * 128 : part * 128 + lanes] = found[:, :lanes]

    def to_sibling(group, k, h, owner):
        slab = fulls[k].at[half(owner, h)]
        passed.append(remote(slab, slab, fsend.at[group, k, h], frecv.at[group, k, h], sibling))

    look_up(0)
    relayed = {}
    for k in range(2):
        for way, target in ((0, right), (1, left)):
            h = way
            first[way, k, h].wait_recv()
            owner = device(3 if way == 0 else 1)
            slab = fulls[k].at[half(owner, h)]
            relayed[way, k] = remote(slab, slab, rsend.at[way, k], rrecv.at[way, k], target)
            to_sibling(1 + way, k, h, owner)
    look_up(1)
    wide = tok_ref[...].astype(F32)
    centered = wide - jnp.mean(wide, axis=-1, keepdims=True)
    inv_sigma = lax.rsqrt(jnp.mean(centered * centered, axis=-1, keepdims=True) + NORM_EPS)
    rounded = (centered * inv_sigma * gain_ref[...]).astype(BF16)
    normed_ref[...] = rounded
    flipped_ref[...] = rounded.T
    for k in range(2):
        for way in range(2):
            first[way, k, 1 - way].wait_recv()
            to_sibling(1 + way, k, 1 - way, device(3 if way == 0 else 1))
    for k in range(2):
        for way in range(2):
            relayed[way, k].wait_recv()
            to_sibling(3, k, way, device(2))
    for copy in own:
        copy.wait()
    for copy in passed:
        copy.wait_recv()
    for copy in started:
        copy.wait_send()


def gather_weights(*operands):
    def dma(*shape):
        return [pltpu.SemaphoreType.DMA(shape)] * 2

    return pl.pallas_call(
        gather_kernel,
        out_shape=(
            jax.ShapeDtypeStruct((WIDTH, 3 * WIDTH), BF16),
            jax.ShapeDtypeStruct((WIDTH, WIDTH), BF16),
            jax.ShapeDtypeStruct((HEADS, SPAN, SPAN), F32),
            jax.ShapeDtypeStruct((ROWS, WIDTH), BF16),
            jax.ShapeDtypeStruct((WIDTH, ROWS), BF16),
        ),
        in_specs=[HBM] * len(operands),
        out_specs=(VMEM,) * 5,
        scratch_shapes=[pltpu.VMEM(a.shape, a.dtype) for a in operands[2:]]
        + [pltpu.VMEM((SPAN, 256), jnp.int32), pltpu.VMEM((HEADS, CHUNKS * 128), F32)]
        + dma(2, 2, 2) + dma(2, 2) + dma(4, 2, 2)
        + [pltpu.SemaphoreType.DMA((6,))],
        compiler_params=pltpu.CompilerParams(collective_id=0, has_side_effects=True, vmem_limit_bytes=32 << 20),
        name="gather_weights",
    )(*(pltpu.with_memory_space_constraint(a, pltpu.HBM) for a in operands))


def orthonormal_rows(left, halfway):
    lane = lax.broadcasted_iota(jnp.int32, (8, 128), 1)
    row = lax.broadcasted_iota(jnp.int32, (8, 128), 0)
    is_in = lane < BLOCK
    zero = jnp.zeros((8, 128), F32)

    def lane_sum(a):
        return jnp.sum(a, axis=1, keepdims=True)

    columns = [left[8 * g : 8 * g + 8, :] for g in range(4)]
    in_columns = [jnp.where(is_in, v, 0.0) for v in columns]
    out_columns = [jnp.where(is_in, 0.0, v) for v in columns]
    taken = [zero] * 4
    in_w, out_w, in_wr, out_wr, squares = ([zero] * 4 for _ in range(5))
    for c in range(32):
        g, at = c // 8, c % 8
        if c == 16:
            halfway()
        here = row == at
        vector = jnp.broadcast_to((columns[g] - taken[g])[at : at + 1, :], (8, 128))
        if c:
            total = None
            for k in range(g + 1):
                term = in_wr[k] * lane_sum(in_w[k] * vector) + out_wr[k] * lane_sum(out_w[k] * vector)
                total = term if total is None else total + term
            vector = vector - jnp.sum(total, axis=0, keepdims=True)
        in_v, out_v = jnp.where(is_in, vector, 0.0), jnp.where(is_in, 0.0, vector)
        square = jnp.where(is_in, lane_sum(in_v * in_v), lane_sum(out_v * out_v))
        share = 1.0 / (square + BASIS_EPS)
        in_scaled, out_scaled = in_v * share, out_v * share
        for k in range(g, 4):
            taken[k] = (
                taken[k] + in_scaled * lane_sum(in_columns[k] * vector) + out_scaled * lane_sum(out_columns[k] * vector)
            )
        in_w[g], out_w[g] = jnp.where(here, in_v, in_w[g]), jnp.where(here, out_v, out_w[g])
        in_wr[g], out_wr[g] = jnp.where(here, in_scaled, in_wr[g]), jnp.where(here, out_scaled, out_wr[g])
        squares[g] = jnp.where(here, square, squares[g])
    return jnp.concatenate([(in_w[g] + out_w[g]) * lax.rsqrt(squares[g] + BASIS_EPS) for g in range(4)], axis=0)


def layer_kernel(
    cot_hbm, region_hbm, in_error_hbm, out_error_hbm, tok_hbm, gain_hbm, bucket_hbm, in_basis_hbm, out_basis_hbm,
    bias_ref, normed, flipped, win_ref, wout_ref,
    tokgrad_ref, merged, mean, extra_all, ortho,
    cot_ref, region_ref, in_error, out_error, tok_ref, gain_ref, bucket_ref, in_basis, out_basis, staging,
    proj, mixgrad, mixed, packed, x_hat, score_high, score_low,
    prod, near, mine, far, out_prod, out_near, out_mine, out_far,
    err_y, err_slab, err_z, err_full,
    sum_src, out_src, sum_own, sum_y, sum_slab, sum_z, sum_full,
    ex, ex_near, ex_mine, ex_far, ex_part, ex_y, ex_z, left_part, left_z, left_all,
    s_near, r_near, s_far, r_far, s_fo, r_fo,
    s_ey, r_ey, s_ez, r_ez, s_ezz, r_ezz, s_eyy, r_eyy,
    s_ty, r_ty, s_tz, r_tz, s_tzz, r_tzz, s_tyy, r_tyy,
    s_xn, r_xn, s_xf, r_xf, s_xy, r_xy, s_xz, r_xz, s_xx, r_xx, s_lz, r_lz, s_ly, r_ly,
):
    dp, mp = lax.axis_index("dp"), lax.axis_index("mp")
    z, y, x, core = dp // N_Y, dp % N_Y, mp // 2, mp % 2
    sibling = {"mp": 2 * x + 1 - core}
    split = 3 * WIDTH

    def x_peer(step):
        return {"mp": 2 * ((x + step) % N_X) + core}

    def y_peer(step):
        return {"dp": z * N_Y + (y + step) % N_Y}

    def z_peer(step):
        return {"dp": ((z + step) % N_Z) * N_Y + y}

    sent = []

    def remote(src, dst, send, recv, target):
        copy = pltpu.make_async_remote_copy(src, dst, send, recv, device_id=target, device_id_type=MESH)
        copy.start()
        sent.append(copy)
        return copy

    def slab_rows(index):
        return pl.ds(pl.multiple_of(index * 16, 16), 16)

    four = (2, 1, 3)
    z_steps = (8, 7, 9, 6, 10, 5, 11, 4, 12, 3, 13, 2, 14, 1, 15)
    near_first = tuple(reversed(z_steps))

    barrier = pltpu.get_barrier_semaphore()
    peers = [z_peer(s) for s in z_steps] + [y_peer(s) for s in four] + [{"mp": (mp + s) % N_MP} for s in range(1, N_MP)]
    for target in peers:
        pl.semaphore_signal(barrier, inc=1, device_id=target, device_id_type=MESH)

    staged = [
        pltpu.make_async_copy(src, dst, staging.at[k])
        for k, (src, dst) in enumerate(
            (
                (cot_hbm, cot_ref), (region_hbm, region_ref), (in_error_hbm, in_error), (out_error_hbm, out_error),
                (tok_hbm, tok_ref), (gain_hbm, gain_ref), (bucket_hbm, bucket_ref),
                (in_basis_hbm, in_basis), (out_basis_hbm, out_basis),
            )
        )
    ]
    for copy in staged:
        copy.start()

    proj[...] = nn(normed[...], win_ref[...]).astype(BF16)
    for copy in staged:
        copy.wait()
    mixgrad[...] = nt(cot_ref[...], wout_ref[...]).astype(BF16)

    lane = lax.broadcasted_iota(jnp.int32, (1, 128), 1)
    first_half = lane < 64
    halves = (first_half.astype(BF16), (lane >= 64).astype(BF16))
    scale = jnp.asarray(0.125, BF16)
    allowed = []
    for w in range(WIN):
        square = jnp.broadcast_to(region_ref[w : w + 1, :].astype(F32), (SPAN, SPAN))
        allowed.append(square == square.T)

    def heads(pair):
        at = [pl.ds(k * WIDTH + pair * 128, 128) for k in range(3)]
        cases = [(w, t) for w in range(WIN) for t in range(2)]
        rows = [pl.ds(w * SPAN, SPAN) for w in range(WIN)]
        q = [proj[r, at[0]] * scale for r in rows]
        key = [proj[r, at[1]] for r in rows]
        value = [proj[r, at[2]] for r in rows]
        key_scaled = [k * scale for k in key]
        grad = [mixgrad[r, at[0]] for r in rows]
        scores = [nt(q[w] * halves[t], key[w]) for w, t in cases]
        prob_grad = [nt(grad[w] * halves[t], value[w]) for w, t in cases]
        scores = [jnp.where(allowed[w], v + bias_ref[2 * pair + t], MASKED) for (w, t), v in zip(cases, scores)]
        tops = [jnp.max(v, axis=-1, keepdims=True) for v in scores]
        exps = [jnp.exp(v - top) for v, top in zip(scores, tops)]
        sums = [jnp.sum(v, axis=-1, keepdims=True) for v in exps]
        prob = [v * (1.0 / total) for v, total in zip(exps, sums)]
        prob_b = [v.astype(BF16) for v in prob]
        weighted = [p * g for p, g in zip(prob, prob_grad)]
        shifts = [jnp.sum(v, axis=-1, keepdims=True) for v in weighted]
        out = [nn(v, value[w]) for (w, t), v in zip(cases, prob_b)]
        value_grad = [tn(v, grad[w]) for (w, t), v in zip(cases, prob_b)]
        score_grad = [p * (g - shift) for p, g, shift in zip(prob, prob_grad, shifts)]
        score_b = [v.astype(BF16) for v in score_grad]
        query_grad = [nn(v, key_scaled[w]) for (w, t), v in zip(cases, score_b)]
        key_grad = [tn(v, q[w]) for (w, t), v in zip(cases, score_b)]
        for w in range(WIN):
            joined = [
                jnp.where(first_half, v[2 * w], v[2 * w + 1]).astype(BF16)
                for v in (query_grad, key_grad, value_grad, out)
            ]
            for k in range(3):
                packed[rows[w], at[k]] = joined[k]
            mixed[rows[w], :] = joined[3]
        grads = [[score_grad[t], score_grad[2 + t]] for t in range(2)]
        for t in range(2):
            total = grads[t][0] + grads[t][1]
            high = total.astype(BF16).astype(F32)
            score_high[2 * pair + t] = high
            score_low[2 * pair + t] = total - high
        return at

    near_in, near_out, far_in = {}, {}, {}

    def send_near(i, at):
        columns = jnp.concatenate([packed[:, at[k]] for k in range(3)], axis=1)
        terms = nn(flipped[...], columns).astype(BF16)
        for m in range(N_MP):
            prod[i, m // 2, m % 2] = terms[m * BLOCK : (m + 1) * BLOCK]
        out_terms = tn(mixed[...], cot_ref[...]).astype(BF16)
        for c in range(2):
            out_prod[i, c] = out_terms[c * BLOCK : (c + 1) * BLOCK]
        near_in[i] = remote(prod.at[i, :, 1 - core], near.at[i], s_near.at[i, 0], r_near.at[i, 0], sibling)
        near_out[i] = remote(out_prod.at[i, 1 - core], out_near.at[i], s_near.at[i, 1], r_near.at[i, 1], sibling)

    def send_far(i):
        near_in[i].wait_recv()
        for s in four:
            chip = (x + s) % N_X
            mine[i, s] = (prod[i, chip, core].astype(F32) + near[i, chip].astype(F32)).astype(BF16)
            far_in[i, s] = remote(mine.at[i, s], far.at[i, s], s_far.at[i, s], r_far.at[i, s], x_peer(s))
        near_out[i].wait_recv()
        out_mine[i] = (out_prod[i, core].astype(F32) + out_near[i].astype(F32)).astype(BF16)
        for s in four:

            @pl.when((x + s) % N_X == i)
            def _(s=s):
                far_out(i, s).start()

    def far_out(i, s):
        return pltpu.make_async_remote_copy(
            out_mine.at[i], out_far.at[s], s_fo.at[s], r_fo.at[s], device_id=x_peer(s), device_id_type=MESH
        )

    e_y = []

    def error_over_y():
        for s in four:
            rows = slab_rows((y + s) % N_Y)
            e_y.append(remote(in_error.at[rows], err_y.at[s, :, pl.ds(0, split)], s_ey.at[s, 0], r_ey.at[s, 0], y_peer(s)))
            e_y.append(
                remote(out_error.at[rows], err_y.at[s, :, pl.ds(split, WIDTH)], s_ey.at[s, 1], r_ey.at[s, 1], y_peer(s))
            )

    for i in range(4):
        at = heads(i)
        if i == 0:
            pl.semaphore_wait(barrier, len(peers))
        send_near(i, at)
        if i == 0:
            error_over_y()
        if i:
            send_far(i - 1)


    for copy in e_y:
        copy.wait_recv()
    err = err_y[1] + err_y[2] + err_y[3]
    err_in = err[:, :split] + in_error[slab_rows(y), :]
    err_out = err[:, split:] + out_error[slab_rows(y), :]
    for k in range(N_Z):
        src = err_in if k < 12 else err_out
        err_slab[k] = src[:, 128 * (k % 12) : 128 * (k % 12) + 128]
    e_z = {s: remote(err_slab.at[(z + s) % N_Z], err_z.at[s], s_ez.at[s], r_ez.at[s], z_peer(s)) for s in z_steps}

    gain = gain_ref[...]
    wide = tok_ref[...].astype(F32)
    centered = wide - jnp.mean(wide, axis=-1, keepdims=True)
    inv_sigma = lax.rsqrt(jnp.mean(centered * centered, axis=-1, keepdims=True) + NORM_EPS)
    x_hat[...] = centered * inv_sigma
    normed_grad = nt(packed[...], win_ref[...])
    gain_term = jnp.sum(normed_grad * x_hat[...], axis=0, keepdims=True)
    hat_grad = normed_grad * gain
    delta = inv_sigma * (
        hat_grad
        - jnp.mean(hat_grad, axis=-1, keepdims=True)
        - x_hat[...] * jnp.mean(hat_grad * x_hat[...], axis=-1, keepdims=True)
    )
    tokgrad_ref[...] = (cot_ref[...].astype(F32) + delta).astype(BF16)

    send_far(3)

    t_y = {}

    def send_y(j, total, src, width):
        src[...] = total.astype(BF16)
        for s in four:
            rows = slab_rows((y + s) % N_Y)
            t_y[j, s] = remote(
                src.at[rows], sum_y.at[j, s, :, pl.ds(0, width)], s_ty.at[j, s], r_ty.at[j, s], y_peer(s)
            )

    def sum_chunk(i):
        total = prod[i, x, core].astype(F32) + near[i, x].astype(F32)
        for s in (1, 3, 2):
            far_in[i, s].wait_recv()
            total = total + far[i, s].astype(F32)
        total = total * (1.0 / N_MP)
        for k in range(3):
            cols = pl.ds(k * WIDTH + i * 128, 128)
            merged[:, cols] = total[:, 128 * k : 128 * (k + 1)] + in_error[:, cols]
        send_y(i, total, sum_src.at[i], 384)
        sum_own[i, :, :384] = total

    for i in range(2):
        sum_chunk(i)

    chunk_row = lax.broadcasted_iota(jnp.int32, (8, SPAN), 0)
    within = lax.broadcasted_iota(jnp.int32, (128, SPAN), 0)

    def add_rows(block, total):
        for k in range(16):
            i = block * 16 + k
            bucket = bucket_ref[pl.ds(i, 1), :]
            chunk_is = jnp.broadcast_to(bucket >> 7, (8, SPAN)) == chunk_row
            one_hot = jnp.where(jnp.broadcast_to(bucket & 127, (128, SPAN)) == within, 1.0, 0.0).astype(BF16)
            picked = jnp.concatenate(
                [
                    jnp.where(chunk_is, jnp.broadcast_to(part[head, pl.ds(i, 1), :], (8, SPAN)), 0.0)
                    for part in (score_high, score_low)
                    for head in range(HEADS)
                ],
                axis=0,
            ).astype(BF16)
            total = total + nt(picked, one_hot)
        return total

    total = lax.fori_loop(0, SPAN // 16, add_rows, jnp.zeros((128, 128), F32))
    table_term = total[:64] + total[64:]
    for head in range(HEADS):
        ex[head // 2, head % 2] = table_term[8 * head : 8 * head + 8]
        part = gain_term[:, 128 * (head // 2) : 128 * (head // 2 + 1)]
        if head % 2:
            part = pltpu.roll(part, 64, 1)
        ex[head // 2, head % 2, 6:7, :] = part
    x_near = {
        s: remote(ex.at[(x + s) % N_X, 1 - core], ex_near.at[s], s_xn.at[s], r_xn.at[s], sibling) for s in (2, 1, 3, 0)
    }

    piece = err_slab[z]
    for s in near_first:
        e_z[s].wait_recv()
        piece = piece + err_z[s]
    err_full[y, z] = piece * (1.0 / (N_Y * N_Z))
    here = err_full.at[y, z]
    e_zz = {s: remote(here, here, s_ezz.at[s], r_ezz.at[s], z_peer(s)) for s in z_steps}

    for i in range(2, 4):
        sum_chunk(i)
    total = out_prod[x, core].astype(F32) + out_near[x].astype(F32)
    for s in (1, 3, 2):
        far_out(0, s).wait_recv()
        total = total + out_far[s].astype(F32)
    total = total * (1.0 / N_MP)
    merged[:, split:] = total + out_error[...]
    send_y(4, total, out_src, WIDTH)
    sum_own[4] = total

    x_far = {}
    for s in four:
        x_near[s].wait_recv()
        ex_mine[s] = ex[(x + s) % N_X, core] + ex_near[s]
        x_far[s] = remote(ex_mine.at[s], ex_far.at[s], s_xf.at[s], r_xf.at[s], x_peer(s))

    for j in range(5):
        total = sum_own[j, slab_rows(y), :]
        for s in (1, 3, 2):
            t_y[j, s].wait_recv()
            total = total + sum_y[j, s].astype(F32)
        for k in range(3 if j < 4 else 4):
            piece_at = 4 * k + j if j < 4 else 12 + k
            sum_slab[piece_at] = total[:, 128 * k : 128 * (k + 1)]
    rounded = sum_slab[...].astype(BF16)
    sum_send = sum_full.at[N_Y]
    sum_full[N_Y] = rounded
    t_z = {s: remote(sum_send.at[(z + s) % N_Z], sum_z.at[s], s_tz.at[s], r_tz.at[s], z_peer(s)) for s in z_steps}

    def left_rows(ref, *at):
        wide = jnp.concatenate([ref[*at, k] for k in range(N_Z)], axis=1)
        both = jnp.concatenate(
            [nt(wide[:, :split], in_basis[...], precision=HIGH), nt(wide[:, split:], out_basis[...], precision=HIGH)],
            axis=1,
        )
        return jnp.concatenate([both[:8], both[8:]], axis=1)

    left = left_rows(sum_slab) * (1.0 / (N_Y * N_Z))
    left_part[...] = left
    l_z = {s: remote(left_part, left_z.at[s], s_lz.at[s], r_lz.at[s], z_peer(s)) for s in z_steps}

    x_near[0].wait_recv()
    part = ex[x, core] + ex_near[0]
    for s in four:
        x_far[s].wait_recv()
        part = part + ex_far[s]
    ex_part[0] = part
    x_y = {s: remote(ex_part.at[0], ex_y.at[s], s_xy.at[s], r_xy.at[s], y_peer(s)) for s in four}

    for s in near_first:
        e_zz[s].wait_recv()
    here = err_full.at[y]
    e_yy = {s: remote(here, here, s_eyy.at[s], r_eyy.at[s], y_peer(s)) for s in four}
    left = left + left_rows(err_full, y)

    for s in four:
        x_y[s].wait_recv()
        part = part + ex_y[s]
    ex_part[1] = part
    x_z = {s: remote(ex_part.at[1], ex_z.at[s], s_xz.at[s], r_xz.at[s], z_peer(s)) for s in z_steps}

    piece = sum_slab[z]
    for s in near_first:
        t_z[s].wait_recv()
        piece = piece + sum_z[s].astype(F32)
    sum_full[y, z] = (piece * (1.0 / (N_Y * N_Z))).astype(BF16)
    here = sum_full.at[y, z]
    t_zz = {s: remote(here, here, s_tzz.at[s], r_tzz.at[s], z_peer(s)) for s in z_steps}

    for s in near_first:
        l_z[s].wait_recv()
        left = left + left_z[s]
    left_all[y] = left
    here = left_all.at[y]
    l_y = {s: remote(here, here, s_ly.at[s], r_ly.at[s], y_peer(s)) for s in four}

    for s in (1, 3, 2):
        l_y[s].wait_recv()
    rows_of = []
    for k in range(N_Y):
        rows_of += [left_all[k, :, :BLOCK], left_all[k, :, BLOCK:]]
    flipped_left = jnp.concatenate(rows_of, axis=0).T

    def finish(slab):
        for k in range(N_Z):
            mean[slab_rows(slab), 128 * k : 128 * (k + 1)] = err_full[slab, k] + sum_full[slab, k].astype(F32)

    t_yy, x_x = {}, {}

    def halfway():
        for s in near_first:
            t_zz[s].wait_recv()
        here = sum_full.at[y]
        for s in four:
            t_yy[s] = remote(here, here, s_tyy.at[s], r_tyy.at[s], y_peer(s))
        total = part
        for s in near_first:
            x_z[s].wait_recv()
            total = total + ex_z[s]
        extra_all[mp] = total
        here = extra_all.at[mp]
        for s in range(1, N_MP):
            x_x[s] = remote(here, here, s_xx.at[s], r_xx.at[s], {"mp": (mp + s) % N_MP})

    ortho[...] = orthonormal_rows(jnp.concatenate([flipped_left[:32], flipped_left[32:]], axis=1), halfway)

    finish(y)
    for s in (1, 3, 2):
        e_yy[s].wait_recv()
        t_yy[s].wait_recv()
        finish((y + N_Y - s) % N_Y)
    for copy in x_x.values():
        copy.wait_recv()
    for s in four:
        far_out(0, s).wait_send()
    for copy in sent:
        copy.wait_send()


def layer(*operands):
    def vmem(*shape, dtype=F32):
        return pltpu.VMEM(shape, dtype)

    def dma(*shape):
        return [pltpu.SemaphoreType.DMA(shape)] * 2

    return pl.pallas_call(
        layer_kernel,
        out_shape=(
            jax.ShapeDtypeStruct((ROWS, WIDTH), BF16),
            jax.ShapeDtypeStruct((BLOCK, COLS), F32),
            jax.ShapeDtypeStruct((BLOCK, COLS), F32),
            jax.ShapeDtypeStruct((N_MP, 8, 128), F32),
            jax.ShapeDtypeStruct((32, 2 * BLOCK), F32),
        ),
        in_specs=[HBM] * 9 + [VMEM] * 5,
        out_specs=(VMEM,) * 5,
        scratch_shapes=[pltpu.VMEM(a.shape, a.dtype) for a in operands[:9]]
        + [pltpu.SemaphoreType.DMA((9,))]
        + [
            vmem(ROWS, 3 * WIDTH, dtype=BF16),
            vmem(ROWS, WIDTH, dtype=BF16),
            vmem(ROWS, 128, dtype=BF16),
            vmem(ROWS, 3 * WIDTH, dtype=BF16),
            vmem(ROWS, WIDTH),
            vmem(HEADS, SPAN, SPAN),
            vmem(HEADS, SPAN, SPAN),
            vmem(4, N_X, 2, BLOCK, 384, dtype=BF16),
            vmem(4, N_X, BLOCK, 384, dtype=BF16),
            vmem(4, N_X, BLOCK, 384, dtype=BF16),
            vmem(4, N_X, BLOCK, 384, dtype=BF16),
            vmem(4, 2, BLOCK, WIDTH, dtype=BF16),
            vmem(4, BLOCK, WIDTH, dtype=BF16),
            vmem(N_X, BLOCK, WIDTH, dtype=BF16),
            vmem(N_X, BLOCK, WIDTH, dtype=BF16),
            vmem(N_Y, 16, COLS),
            vmem(N_Z, 16, 128),
            vmem(N_Z, 16, 128),
            vmem(N_Y, N_Z, 16, 128),
            vmem(4, BLOCK, 384, dtype=BF16),
            vmem(BLOCK, WIDTH, dtype=BF16),
            vmem(5, BLOCK, WIDTH),
            vmem(5, N_Y, 16, WIDTH, dtype=BF16),
            vmem(N_Z, 16, 128),
            vmem(N_Z, 16, 128, dtype=BF16),
            vmem(N_Y + 1, N_Z, 16, 128, dtype=BF16),
            vmem(N_X, 2, 8, 128),
            vmem(N_X, 8, 128),
            vmem(N_X, 8, 128),
            vmem(N_X, 8, 128),
            vmem(2, 8, 128),
            vmem(N_Y, 8, 128),
            vmem(N_Z, 8, 128),
            vmem(8, 128),
            vmem(N_Z, 8, 128),
            vmem(N_Y, 8, 128),
        ]
        + dma(4, 2) + dma(4, 4) + dma(4)
        + dma(4, 2) + dma(N_Z) + dma(N_Z) + dma(4)
        + dma(5, 4) + dma(N_Z) + dma(N_Z) + dma(4)
        + dma(4) + dma(4) + dma(4) + dma(N_Z) + dma(N_MP) + dma(N_Z) + dma(4),
        compiler_params=pltpu.CompilerParams(collective_id=1, has_side_effects=True, vmem_limit_bytes=48 << 20),
        name="layer",
    )(*(pltpu.with_memory_space_constraint(a, pltpu.HBM) for a in operands[:9]), *operands[9:])


def factor_kernel(
    mean, merged, ortho, extra, token_grad_in,
    in_update, out_update, in_error, out_error, in_right, out_right, gain_grad, table_grad, token_grad,
):
    split = 3 * WIDTH
    in_ortho, out_ortho = ortho[:, :BLOCK], ortho[:, BLOCK:]
    right = nn(in_ortho, mean[:, :split], precision=HIGH)
    in_right[...] = right
    update = tn(in_ortho, right, precision=HIGH)
    in_update[...] = update
    in_error[...] = merged[:, :split] - update
    right = nn(out_ortho, mean[:, split:], precision=HIGH)
    out_right[...] = right
    update = tn(out_ortho, right, precision=HIGH)
    out_update[...] = update
    out_error[...] = merged[:, split:] - update

    share = 1.0 / (N_Y * N_Z * N_MP)
    buckets = table_grad.shape[1]
    for head in range(HEADS):
        for c in range(CHUNKS):
            width = min(128, buckets - 128 * c)
            table_grad[head : head + 1, 128 * c : 128 * c + width] = extra[head, c : c + 1, :width] * share
    for pair in range(HEADS // 2):
        low, high = extra[2 * pair, 6:7, :], pltpu.roll(extra[2 * pair + 1, 6:7, :], 64, 1)
        lane = lax.broadcasted_iota(jnp.int32, (1, 128), 1)
        gain_grad[:, 128 * pair : 128 * (pair + 1)] = jnp.where(lane < 64, low, high) * share
    token_grad[...] = token_grad_in[...]


def factors(buckets, *operands):
    wide = jax.ShapeDtypeStruct((BLOCK, 3 * WIDTH), F32)
    thin = jax.ShapeDtypeStruct((BLOCK, WIDTH), F32)
    return pl.pallas_call(
        factor_kernel,
        out_shape=(
            wide, thin, wide, thin,
            jax.ShapeDtypeStruct((32, 3 * WIDTH), F32),
            jax.ShapeDtypeStruct((32, WIDTH), F32),
            jax.ShapeDtypeStruct((1, WIDTH), F32),
            jax.ShapeDtypeStruct((HEADS, buckets), F32),
            jax.ShapeDtypeStruct((ROWS, WIDTH), BF16),
        ),
        in_specs=[VMEM] * len(operands),
        out_specs=(VMEM,) * 9,
        compiler_params=pltpu.CompilerParams(vmem_limit_bytes=32 << 20),
        name="factors",
    )(*operands)


def shards(
    tokens,
    cotangent,
    region_ids,
    rel_bucket,
    norm_gain,
    in_weight,
    out_weight,
    bias_table,
    in_error,
    out_error,
    in_basis,
    out_basis,
):
    tok = tokens.reshape(ROWS, WIDTH)
    gain = norm_gain.reshape(1, WIDTH)
    full_in, full_out, bias, normed, flipped = gather_weights(in_weight, out_weight, bias_table, rel_bucket, tok, gain)
    token_grad, merged, mean, extra_all, ortho = layer(
        cotangent.reshape(ROWS, WIDTH), region_ids, in_error[0], out_error[0], tok, gain, rel_bucket,
        in_basis[0].T, out_basis[0].T,
        bias, normed, flipped, full_in, full_out,
    )
    in_update, out_update, in_new, out_new, in_right, out_right, gain_grad, table_grad, token_grad = factors(
        bias_table.shape[1], mean, merged, ortho, extra_all, token_grad
    )
    return (
        token_grad.reshape(tokens.shape),
        gain_grad.reshape(WIDTH),
        table_grad,
        in_update,
        out_update,
        in_new[None],
        out_new[None],
        in_right.T[None],
        out_right.T[None],
    )


def solution(mesh):
    placed = (
        P(("dp", "mp"), None, None),
        P(("dp", "mp"), None, None),
        P(("dp", "mp"), None),
        P(),
        P(),
        P("mp", None),
        P("mp", None),
        P(),
        P("dp", "mp", None),
        P("dp", "mp", None),
        P("mp", None, None),
        P("mp", None, None),
    )
    return jax.shard_map(
        shards,
        mesh=mesh,
        in_specs=placed,
        out_specs=(
            P(("dp", "mp"), None, None),
            P(),
            P(),
            P("mp", None),
            P("mp", None),
            P("dp", "mp", None),
            P("dp", "mp", None),
            P("mp", None, None),
            P("mp", None, None),
        ),
        check_vma=False,
    )
```

```python
import jax
import jax.numpy as jnp
from jax import lax
from jax.experimental import pallas as pl
from jax.experimental.pallas import tpu as pltpu
from jax.sharding import PartitionSpec as P

NORM_EPS = 1e-05
BASIS_EPS = 1e-06
MASKED = -1e30
HIGH = lax.Precision.HIGHEST
MESH = pl.DeviceIdType.MESH
F32 = jnp.float32
BF16 = jnp.bfloat16
VMEM = pl.BlockSpec(memory_space=pltpu.VMEM)
HBM = pl.BlockSpec(memory_space=pltpu.HBM)

WIN, SPAN, WIDTH, HEADS, CHUNKS = 2, 144, 512, 8, 6
ROWS = WIN * SPAN
N_X, N_Y, N_Z, N_MP = 4, 4, 16, 8
BLOCK = 64
COLS = 4 * WIDTH


def nt(a, b, **kw):
    return lax.dot_general(a, b, (((1,), (1,)), ((), ())), preferred_element_type=F32, **kw)


def tn(a, b, **kw):
    return lax.dot_general(a, b, (((0,), (0,)), ((), ())), preferred_element_type=F32, **kw)


def nn(a, b, **kw):
    return jnp.dot(a, b, preferred_element_type=F32, **kw)


def gather_kernel(
    in_ref, out_ref, table_hbm, bucket_hbm, tok_hbm, gain_hbm,
    full_in, full_out, bias_ref, normed_ref, flipped_ref,
    table_ref, bucket_ref, tok_ref, gain_ref, index, table, send, recv, rsend, rrecv, fsend, frecv, local,
):
    mp = lax.axis_index("mp")
    x, core = mp // 2, mp % 2
    sibling = {"mp": 2 * x + 1 - core}

    def device(step):
        return 2 * ((x + step) % N_X) + core

    right, left = {"mp": device(1)}, {"mp": device(3)}
    barrier = pltpu.get_barrier_semaphore()
    for target in (right, left, sibling):
        pl.semaphore_signal(barrier, inc=1, device_id=target, device_id_type=MESH)

    sources, fulls = (in_ref, out_ref), (full_in, full_out)
    half_rows = BLOCK // 2

    def rows(owner):
        return pl.ds(pl.multiple_of(owner * BLOCK, BLOCK), BLOCK)

    def half(owner, h):
        return pl.ds(pl.multiple_of(owner * BLOCK + h * half_rows, half_rows), half_rows)

    own = [pltpu.make_async_copy(sources[k], fulls[k].at[rows(mp)], local.at[k]) for k in range(2)]
    staged = [
        pltpu.make_async_copy(src, dst, local.at[2 + k])
        for k, (src, dst) in enumerate(
            ((table_hbm, table_ref), (bucket_hbm, bucket_ref), (tok_hbm, tok_ref), (gain_hbm, gain_ref))
        )
    ]
    for copy in staged + own:
        copy.start()
    for copy in staged:
        copy.wait()
    index[...] = jnp.zeros_like(index)
    index[:, :SPAN] = bucket_ref[...]
    table[...] = jnp.zeros_like(table)
    table[:, : table_ref.shape[1]] = table_ref[...]
    pl.semaphore_wait(barrier, 3)

    started = []

    def remote(src, dst, send_sem, recv_sem, target):
        copy = pltpu.make_async_remote_copy(src, dst, send_sem, recv_sem, device_id=target, device_id_type=MESH)
        copy.start()
        started.append(copy)
        return copy

    first = {}
    for turn in range(2):
        for k in range(2):
            for way, target in ((0, right), (1, left)):
                h = turn ^ way
                first[way, k, h] = remote(
                    sources[k].at[pl.ds(h * half_rows, half_rows)], fulls[k].at[half(mp, h)],
                    send.at[way, k, h], recv.at[way, k, h], target,
                )
    passed = [
        remote(sources[k], fulls[k].at[rows(mp)], fsend.at[0, k, 0], frecv.at[0, k, 0], sibling) for k in range(2)
    ]

    def look_up(part):
        lanes = 128 if part == 0 else SPAN - 128

        @pl.loop(0, SPAN // 16)
        def _(block):
            at = pl.ds(pl.multiple_of(block * 16, 16), 16)
            bucket = index[at, pl.ds(part * 128, 128)]
            low = bucket & 127
            chunk = bucket >> 7
            for head in range(HEADS):
                found = jnp.zeros((16, 128), F32)
                for c in range(CHUNKS):
                    row = jnp.broadcast_to(table[head : head + 1, c * 128 : (c + 1) * 128], (16, 128))
                    found = jnp.where(chunk == c, jnp.take_along_axis(row, low, axis=1), found)
                bias_ref[head, at, part * 128 : part * 128 + lanes] = found[:, :lanes]

    def to_sibling(group, k, h, owner):
        slab = fulls[k].at[half(owner, h)]
        passed.append(remote(slab, slab, fsend.at[group, k, h], frecv.at[group, k, h], sibling))

    look_up(0)
    relayed = {}
    for k in range(2):
        for way, target in ((0, right), (1, left)):
            h = way
            first[way, k, h].wait_recv()
            owner = device(3 if way == 0 else 1)
            slab = fulls[k].at[half(owner, h)]
            relayed[way, k] = remote(slab, slab, rsend.at[way, k], rrecv.at[way, k], target)
            to_sibling(1 + way, k, h, owner)
    look_up(1)
    wide = tok_ref[...].astype(F32)
    centered = wide - jnp.mean(wide, axis=-1, keepdims=True)
    inv_sigma = lax.rsqrt(jnp.mean(centered * centered, axis=-1, keepdims=True) + NORM_EPS)
    rounded = (centered * inv_sigma * gain_ref[...]).astype(BF16)
    normed_ref[...] = rounded
    flipped_ref[...] = rounded.T
    for k in range(2):
        for way in range(2):
            first[way, k, 1 - way].wait_recv()
            to_sibling(1 + way, k, 1 - way, device(3 if way == 0 else 1))
    for k in range(2):
        for way in range(2):
            relayed[way, k].wait_recv()
            to_sibling(3, k, way, device(2))
    for copy in own:
        copy.wait()
    for copy in passed:
        copy.wait_recv()
    for copy in started:
        copy.wait_send()


def gather_weights(*operands):
    def dma(*shape):
        return [pltpu.SemaphoreType.DMA(shape)] * 2

    return pl.pallas_call(
        gather_kernel,
        out_shape=(
            jax.ShapeDtypeStruct((WIDTH, 3 * WIDTH), BF16),
            jax.ShapeDtypeStruct((WIDTH, WIDTH), BF16),
            jax.ShapeDtypeStruct((HEADS, SPAN, SPAN), F32),
            jax.ShapeDtypeStruct((ROWS, WIDTH), BF16),
            jax.ShapeDtypeStruct((WIDTH, ROWS), BF16),
        ),
        in_specs=[HBM] * len(operands),
        out_specs=(VMEM,) * 5,
        scratch_shapes=[pltpu.VMEM(a.shape, a.dtype) for a in operands[2:]]
        + [pltpu.VMEM((SPAN, 256), jnp.int32), pltpu.VMEM((HEADS, CHUNKS * 128), F32)]
        + dma(2, 2, 2) + dma(2, 2) + dma(4, 2, 2)
        + [pltpu.SemaphoreType.DMA((6,))],
        compiler_params=pltpu.CompilerParams(collective_id=0, has_side_effects=True, vmem_limit_bytes=32 << 20),
        name="gather_weights",
    )(*(pltpu.with_memory_space_constraint(a, pltpu.HBM) for a in operands))


def orthonormal_rows(left, halfway):
    lane = lax.broadcasted_iota(jnp.int32, (8, 128), 1)
    row = lax.broadcasted_iota(jnp.int32, (8, 128), 0)
    is_in = lane < BLOCK
    zero = jnp.zeros((8, 128), F32)

    def lane_sum(a):
        return jnp.sum(a, axis=1, keepdims=True)

    columns = [left[8 * g : 8 * g + 8, :] for g in range(4)]
    in_columns = [jnp.where(is_in, v, 0.0) for v in columns]
    out_columns = [jnp.where(is_in, 0.0, v) for v in columns]
    taken = [zero] * 4
    in_w, out_w, in_wr, out_wr, squares = ([zero] * 4 for _ in range(5))
    for c in range(32):
        g, at = c // 8, c % 8
        if c == 8:
            halfway()
        here = row == at
        vector = jnp.broadcast_to((columns[g] - taken[g])[at : at + 1, :], (8, 128))
        if c:
            total = None
            for k in range(g + 1):
                term = in_wr[k] * lane_sum(in_w[k] * vector) + out_wr[k] * lane_sum(out_w[k] * vector)
                total = term if total is None else total + term
            vector = vector - jnp.sum(total, axis=0, keepdims=True)
        in_v, out_v = jnp.where(is_in, vector, 0.0), jnp.where(is_in, 0.0, vector)
        square = jnp.where(is_in, lane_sum(in_v * in_v), lane_sum(out_v * out_v))
        share = 1.0 / (square + BASIS_EPS)
        in_scaled, out_scaled = in_v * share, out_v * share
        for k in range(g, 4):
            taken[k] = (
                taken[k] + in_scaled * lane_sum(in_columns[k] * vector) + out_scaled * lane_sum(out_columns[k] * vector)
            )
        in_w[g], out_w[g] = jnp.where(here, in_v, in_w[g]), jnp.where(here, out_v, out_w[g])
        in_wr[g], out_wr[g] = jnp.where(here, in_scaled, in_wr[g]), jnp.where(here, out_scaled, out_wr[g])
        squares[g] = jnp.where(here, square, squares[g])
    return jnp.concatenate([(in_w[g] + out_w[g]) * lax.rsqrt(squares[g] + BASIS_EPS) for g in range(4)], axis=0)


def layer_kernel(
    cot_hbm, region_hbm, in_error_hbm, out_error_hbm, tok_hbm, gain_hbm, bucket_hbm, in_basis_hbm, out_basis_hbm,
    bias_ref, normed, flipped, win_ref, wout_ref,
    tokgrad_ref, merged, mean, extra_all, ortho,
    cot_ref, region_ref, in_error, out_error, tok_ref, gain_ref, bucket_ref, in_basis, out_basis, staging,
    proj, mixgrad, mixed, packed, x_hat, score_high, score_low,
    prod, near, mine, far, out_prod, out_near, out_mine, out_far,
    err_y, err_slab, err_z, err_full,
    sum_src, out_src, sum_own, sum_y, sum_slab, sum_z, sum_full,
    ex, ex_near, ex_mine, ex_far, ex_part, ex_y, ex_z, left_part, left_z, left_all,
    s_near, r_near, s_far, r_far, s_fo, r_fo,
    s_ey, r_ey, s_ez, r_ez, s_ezz, r_ezz, s_eyy, r_eyy,
    s_ty, r_ty, s_tz, r_tz, s_tzz, r_tzz, s_tyy, r_tyy,
    s_xn, r_xn, s_xf, r_xf, s_xy, r_xy, s_xz, r_xz, s_xx, r_xx, s_lz, r_lz, s_ly, r_ly,
):
    dp, mp = lax.axis_index("dp"), lax.axis_index("mp")
    z, y, x, core = dp // N_Y, dp % N_Y, mp // 2, mp % 2
    sibling = {"mp": 2 * x + 1 - core}
    split = 3 * WIDTH

    def x_peer(step):
        return {"mp": 2 * ((x + step) % N_X) + core}

    def y_peer(step):
        return {"dp": z * N_Y + (y + step) % N_Y}

    def z_peer(step):
        return {"dp": ((z + step) % N_Z) * N_Y + y}

    sent = []

    def remote(src, dst, send, recv, target):
        copy = pltpu.make_async_remote_copy(src, dst, send, recv, device_id=target, device_id_type=MESH)
        copy.start()
        sent.append(copy)
        return copy

    def slab_rows(index):
        return pl.ds(pl.multiple_of(index * 16, 16), 16)

    four = (2, 1, 3)
    z_steps = (8, 7, 9, 6, 10, 5, 11, 4, 12, 3, 13, 2, 14, 1, 15)
    near_first = tuple(reversed(z_steps))

    barrier = pltpu.get_barrier_semaphore()
    peers = [z_peer(s) for s in z_steps] + [y_peer(s) for s in four] + [{"mp": (mp + s) % N_MP} for s in range(1, N_MP)]
    for target in peers:
        pl.semaphore_signal(barrier, inc=1, device_id=target, device_id_type=MESH)

    staged = [
        pltpu.make_async_copy(src, dst, staging.at[k])
        for k, (src, dst) in enumerate(
            (
                (cot_hbm, cot_ref), (region_hbm, region_ref), (in_error_hbm, in_error), (out_error_hbm, out_error),
                (tok_hbm, tok_ref), (gain_hbm, gain_ref), (bucket_hbm, bucket_ref),
                (in_basis_hbm, in_basis), (out_basis_hbm, out_basis),
            )
        )
    ]
    for copy in staged:
        copy.start()

    proj[...] = nn(normed[...], win_ref[...]).astype(BF16)
    for copy in staged:
        copy.wait()
    mixgrad[...] = nt(cot_ref[...], wout_ref[...]).astype(BF16)

    lane = lax.broadcasted_iota(jnp.int32, (1, 128), 1)
    first_half = lane < 64
    halves = (first_half.astype(BF16), (lane >= 64).astype(BF16))
    scale = jnp.asarray(0.125, BF16)
    allowed = []
    for w in range(WIN):
        square = jnp.broadcast_to(region_ref[w : w + 1, :].astype(F32), (SPAN, SPAN))
        allowed.append(square == square.T)

    def heads(pair):
        at = [pl.ds(k * WIDTH + pair * 128, 128) for k in range(3)]
        cases = [(w, t) for w in range(WIN) for t in range(2)]
        rows = [pl.ds(w * SPAN, SPAN) for w in range(WIN)]
        q = [proj[r, at[0]] * scale for r in rows]
        key = [proj[r, at[1]] for r in rows]
        value = [proj[r, at[2]] for r in rows]
        key_scaled = [k * scale for k in key]
        grad = [mixgrad[r, at[0]] for r in rows]
        scores = [nt(q[w] * halves[t], key[w]) for w, t in cases]
        prob_grad = [nt(grad[w] * halves[t], value[w]) for w, t in cases]
        scores = [jnp.where(allowed[w], v + bias_ref[2 * pair + t], MASKED) for (w, t), v in zip(cases, scores)]
        tops = [jnp.max(v, axis=-1, keepdims=True) for v in scores]
        exps = [jnp.exp(v - top) for v, top in zip(scores, tops)]
        sums = [jnp.sum(v, axis=-1, keepdims=True) for v in exps]
        prob = [v * (1.0 / total) for v, total in zip(exps, sums)]
        prob_b = [v.astype(BF16) for v in prob]
        weighted = [p * g for p, g in zip(prob, prob_grad)]
        shifts = [jnp.sum(v, axis=-1, keepdims=True) for v in weighted]
        out = [nn(v, value[w]) for (w, t), v in zip(cases, prob_b)]
        value_grad = [tn(v, grad[w]) for (w, t), v in zip(cases, prob_b)]
        score_grad = [p * (g - shift) for p, g, shift in zip(prob, prob_grad, shifts)]
        score_b = [v.astype(BF16) for v in score_grad]
        query_grad = [nn(v, key_scaled[w]) for (w, t), v in zip(cases, score_b)]
        key_grad = [tn(v, q[w]) for (w, t), v in zip(cases, score_b)]
        for w in range(WIN):
            joined = [
                jnp.where(first_half, v[2 * w], v[2 * w + 1]).astype(BF16)
                for v in (query_grad, key_grad, value_grad, out)
            ]
            for k in range(3):
                packed[rows[w], at[k]] = joined[k]
            mixed[rows[w], :] = joined[3]
        grads = [[score_grad[t], score_grad[2 + t]] for t in range(2)]
        for t in range(2):
            total = grads[t][0] + grads[t][1]
            high = total.astype(BF16).astype(F32)
            score_high[2 * pair + t] = high
            score_low[2 * pair + t] = total - high
        return at

    near_in, near_out, far_in = {}, {}, {}

    def send_near(i, at):
        columns = jnp.concatenate([packed[:, at[k]] for k in range(3)], axis=1)
        terms = nn(flipped[...], columns).astype(BF16)
        for m in range(N_MP):
            prod[i, m // 2, m % 2] = terms[m * BLOCK : (m + 1) * BLOCK]
        out_terms = tn(mixed[...], cot_ref[...]).astype(BF16)
        for c in range(2):
            out_prod[i, c] = out_terms[c * BLOCK : (c + 1) * BLOCK]
        near_in[i] = remote(prod.at[i, :, 1 - core], near.at[i], s_near.at[i, 0], r_near.at[i, 0], sibling)
        near_out[i] = remote(out_prod.at[i, 1 - core], out_near.at[i], s_near.at[i, 1], r_near.at[i, 1], sibling)

    def send_far(i):
        near_in[i].wait_recv()
        for s in four:
            chip = (x + s) % N_X
            mine[i, s] = (prod[i, chip, core].astype(F32) + near[i, chip].astype(F32)).astype(BF16)
            far_in[i, s] = remote(mine.at[i, s], far.at[i, s], s_far.at[i, s], r_far.at[i, s], x_peer(s))
        near_out[i].wait_recv()
        out_mine[i] = (out_prod[i, core].astype(F32) + out_near[i].astype(F32)).astype(BF16)
        for s in four:

            @pl.when((x + s) % N_X == i)
            def _(s=s):
                far_out(i, s).start()

    def far_out(i, s):
        return pltpu.make_async_remote_copy(
            out_mine.at[i], out_far.at[s], s_fo.at[s], r_fo.at[s], device_id=x_peer(s), device_id_type=MESH
        )

    e_y = []

    def error_over_y():
        for s in four:
            rows = slab_rows((y + s) % N_Y)
            e_y.append(remote(in_error.at[rows], err_y.at[s, :, pl.ds(0, split)], s_ey.at[s, 0], r_ey.at[s, 0], y_peer(s)))
            e_y.append(
                remote(out_error.at[rows], err_y.at[s, :, pl.ds(split, WIDTH)], s_ey.at[s, 1], r_ey.at[s, 1], y_peer(s))
            )

    pl.semaphore_wait(barrier, len(peers))
    error_over_y()
    for i in range(4):
        at = heads(i)
        send_near(i, at)
        if i:
            send_far(i - 1)


    for copy in e_y:
        copy.wait_recv()
    err = err_y[1] + err_y[2] + err_y[3]
    err_in = err[:, :split] + in_error[slab_rows(y), :]
    err_out = err[:, split:] + out_error[slab_rows(y), :]
    for k in range(N_Z):
        src = err_in if k < 12 else err_out
        err_slab[k] = src[:, 128 * (k % 12) : 128 * (k % 12) + 128]
    e_z = {s: remote(err_slab.at[(z + s) % N_Z], err_z.at[s], s_ez.at[s], r_ez.at[s], z_peer(s)) for s in z_steps}

    gain = gain_ref[...]
    wide = tok_ref[...].astype(F32)
    centered = wide - jnp.mean(wide, axis=-1, keepdims=True)
    inv_sigma = lax.rsqrt(jnp.mean(centered * centered, axis=-1, keepdims=True) + NORM_EPS)
    x_hat[...] = centered * inv_sigma
    normed_grad = nt(packed[...], win_ref[...])
    gain_term = jnp.sum(normed_grad * x_hat[...], axis=0, keepdims=True)
    hat_grad = normed_grad * gain
    delta = inv_sigma * (
        hat_grad
        - jnp.mean(hat_grad, axis=-1, keepdims=True)
        - x_hat[...] * jnp.mean(hat_grad * x_hat[...], axis=-1, keepdims=True)
    )
    tokgrad_ref[...] = (cot_ref[...].astype(F32) + delta).astype(BF16)

    send_far(3)

    t_y = {}

    def send_y(j, total, src, width):
        src[...] = total.astype(BF16)
        for s in four:
            rows = slab_rows((y + s) % N_Y)
            t_y[j, s] = remote(
                src.at[rows], sum_y.at[j, s, :, pl.ds(0, width)], s_ty.at[j, s], r_ty.at[j, s], y_peer(s)
            )

    def sum_chunk(i):
        total = prod[i, x, core].astype(F32) + near[i, x].astype(F32)
        for s in (1, 3, 2):
            far_in[i, s].wait_recv()
            total = total + far[i, s].astype(F32)
        total = total * (1.0 / N_MP)
        for k in range(3):
            cols = pl.ds(k * WIDTH + i * 128, 128)
            merged[:, cols] = total[:, 128 * k : 128 * (k + 1)] + in_error[:, cols]
        send_y(i, total, sum_src.at[i], 384)
        sum_own[i, :, :384] = total

    for i in range(2):
        sum_chunk(i)

    chunk_row = lax.broadcasted_iota(jnp.int32, (8, SPAN), 0)
    within = lax.broadcasted_iota(jnp.int32, (128, SPAN), 0)

    def add_rows(block, total):
        for k in range(16):
            i = block * 16 + k
            bucket = bucket_ref[pl.ds(i, 1), :]
            chunk_is = jnp.broadcast_to(bucket >> 7, (8, SPAN)) == chunk_row
            one_hot = jnp.where(jnp.broadcast_to(bucket & 127, (128, SPAN)) == within, 1.0, 0.0).astype(BF16)
            picked = jnp.concatenate(
                [
                    jnp.where(chunk_is, jnp.broadcast_to(part[head, pl.ds(i, 1), :], (8, SPAN)), 0.0)
                    for part in (score_high, score_low)
                    for head in range(HEADS)
                ],
                axis=0,
            ).astype(BF16)
            total = total + nt(picked, one_hot)
        return total

    total = lax.fori_loop(0, SPAN // 16, add_rows, jnp.zeros((128, 128), F32))
    table_term = total[:64] + total[64:]
    for head in range(HEADS):
        ex[head // 2, head % 2] = table_term[8 * head : 8 * head + 8]
        part = gain_term[:, 128 * (head // 2) : 128 * (head // 2 + 1)]
        if head % 2:
            part = pltpu.roll(part, 64, 1)
        ex[head // 2, head % 2, 6:7, :] = part
    x_near = {
        s: remote(ex.at[(x + s) % N_X, 1 - core], ex_near.at[s], s_xn.at[s], r_xn.at[s], sibling) for s in (2, 1, 3, 0)
    }

    piece = err_slab[z]
    for s in near_first:
        e_z[s].wait_recv()
        piece = piece + err_z[s]
    err_full[y, z] = piece * (1.0 / (N_Y * N_Z))
    here = err_full.at[y, z]
    e_zz = {s: remote(here, here, s_ezz.at[s], r_ezz.at[s], z_peer(s)) for s in z_steps}

    for i in range(2, 4):
        sum_chunk(i)
    total = out_prod[x, core].astype(F32) + out_near[x].astype(F32)
    for s in (1, 3, 2):
        far_out(0, s).wait_recv()
        total = total + out_far[s].astype(F32)
    total = total * (1.0 / N_MP)
    merged[:, split:] = total + out_error[...]
    send_y(4, total, out_src, WIDTH)
    sum_own[4] = total

    x_far = {}
    for s in four:
        x_near[s].wait_recv()
        ex_mine[s] = ex[(x + s) % N_X, core] + ex_near[s]
        x_far[s] = remote(ex_mine.at[s], ex_far.at[s], s_xf.at[s], r_xf.at[s], x_peer(s))

    for j in range(5):
        total = sum_own[j, slab_rows(y), :]
        for s in (1, 3, 2):
            t_y[j, s].wait_recv()
            total = total + sum_y[j, s].astype(F32)
        for k in range(3 if j < 4 else 4):
            piece_at = 4 * k + j if j < 4 else 12 + k
            sum_slab[piece_at] = total[:, 128 * k : 128 * (k + 1)]
    rounded = sum_slab[...].astype(BF16)
    sum_send = sum_full.at[N_Y]
    sum_full[N_Y] = rounded
    t_z = {s: remote(sum_send.at[(z + s) % N_Z], sum_z.at[s], s_tz.at[s], r_tz.at[s], z_peer(s)) for s in z_steps}

    wide = jnp.concatenate([sum_slab[k] + err_slab[k] for k in range(N_Z)], axis=1)
    both = jnp.concatenate(
        [nt(wide[:, :split], in_basis[...], precision=HIGH), nt(wide[:, split:], out_basis[...], precision=HIGH)],
        axis=1,
    )
    left = jnp.concatenate([both[:8], both[8:]], axis=1) * (1.0 / (N_Y * N_Z))
    left_part[...] = left
    l_z = {s: remote(left_part, left_z.at[s], s_lz.at[s], r_lz.at[s], z_peer(s)) for s in z_steps}

    x_near[0].wait_recv()
    part = ex[x, core] + ex_near[0]
    for s in four:
        x_far[s].wait_recv()
        part = part + ex_far[s]
    ex_part[0] = part
    x_y = {s: remote(ex_part.at[0], ex_y.at[s], s_xy.at[s], r_xy.at[s], y_peer(s)) for s in four}

    for s in near_first:
        e_zz[s].wait_recv()
    here = err_full.at[y]
    e_yy = {s: remote(here, here, s_eyy.at[s], r_eyy.at[s], y_peer(s)) for s in four}

    for s in four:
        x_y[s].wait_recv()
        part = part + ex_y[s]
    ex_part[1] = part
    x_z = {s: remote(ex_part.at[1], ex_z.at[s], s_xz.at[s], r_xz.at[s], z_peer(s)) for s in z_steps}

    piece = sum_slab[z]
    for s in near_first:
        t_z[s].wait_recv()
        piece = piece + sum_z[s].astype(F32)
    sum_full[y, z] = (piece * (1.0 / (N_Y * N_Z))).astype(BF16)
    here = sum_full.at[y, z]
    t_zz = {s: remote(here, here, s_tzz.at[s], r_tzz.at[s], z_peer(s)) for s in z_steps}

    for s in near_first:
        l_z[s].wait_recv()
        left = left + left_z[s]
    left_all[y] = left
    here = left_all.at[y]
    l_y = {s: remote(here, here, s_ly.at[s], r_ly.at[s], y_peer(s)) for s in four}

    for s in (1, 3, 2):
        l_y[s].wait_recv()
    rows_of = []
    for k in range(N_Y):
        rows_of += [left_all[k, :, :BLOCK], left_all[k, :, BLOCK:]]
    flipped_left = jnp.concatenate(rows_of, axis=0).T

    def finish(slab):
        for k in range(N_Z):
            mean[slab_rows(slab), 128 * k : 128 * (k + 1)] = err_full[slab, k] + sum_full[slab, k].astype(F32)

    t_yy, x_x = {}, {}

    def halfway():
        for s in near_first:
            t_zz[s].wait_recv()
        here = sum_full.at[y]
        for s in four:
            t_yy[s] = remote(here, here, s_tyy.at[s], r_tyy.at[s], y_peer(s))
        total = part
        for s in near_first:
            x_z[s].wait_recv()
            total = total + ex_z[s]
        extra_all[mp] = total
        here = extra_all.at[mp]
        for s in range(1, N_MP):
            x_x[s] = remote(here, here, s_xx.at[s], r_xx.at[s], {"mp": (mp + s) % N_MP})

    ortho[...] = orthonormal_rows(jnp.concatenate([flipped_left[:32], flipped_left[32:]], axis=1), halfway)

    finish(y)
    for s in (1, 3, 2):
        e_yy[s].wait_recv()
        t_yy[s].wait_recv()
        finish((y + N_Y - s) % N_Y)
    for copy in x_x.values():
        copy.wait_recv()
    for s in four:
        far_out(0, s).wait_send()
    for copy in sent:
        copy.wait_send()


def layer(*operands):
    def vmem(*shape, dtype=F32):
        return pltpu.VMEM(shape, dtype)

    def dma(*shape):
        return [pltpu.SemaphoreType.DMA(shape)] * 2

    return pl.pallas_call(
        layer_kernel,
        out_shape=(
            jax.ShapeDtypeStruct((ROWS, WIDTH), BF16),
            jax.ShapeDtypeStruct((BLOCK, COLS), F32),
            jax.ShapeDtypeStruct((BLOCK, COLS), F32),
            jax.ShapeDtypeStruct((N_MP, 8, 128), F32),
            jax.ShapeDtypeStruct((32, 2 * BLOCK), F32),
        ),
        in_specs=[HBM] * 9 + [VMEM] * 5,
        out_specs=(VMEM,) * 5,
        scratch_shapes=[pltpu.VMEM(a.shape, a.dtype) for a in operands[:9]]
        + [pltpu.SemaphoreType.DMA((9,))]
        + [
            vmem(ROWS, 3 * WIDTH, dtype=BF16),
            vmem(ROWS, WIDTH, dtype=BF16),
            vmem(ROWS, 128, dtype=BF16),
            vmem(ROWS, 3 * WIDTH, dtype=BF16),
            vmem(ROWS, WIDTH),
            vmem(HEADS, SPAN, SPAN),
            vmem(HEADS, SPAN, SPAN),
            vmem(4, N_X, 2, BLOCK, 384, dtype=BF16),
            vmem(4, N_X, BLOCK, 384, dtype=BF16),
            vmem(4, N_X, BLOCK, 384, dtype=BF16),
            vmem(4, N_X, BLOCK, 384, dtype=BF16),
            vmem(4, 2, BLOCK, WIDTH, dtype=BF16),
            vmem(4, BLOCK, WIDTH, dtype=BF16),
            vmem(N_X, BLOCK, WIDTH, dtype=BF16),
            vmem(N_X, BLOCK, WIDTH, dtype=BF16),
            vmem(N_Y, 16, COLS),
            vmem(N_Z, 16, 128),
            vmem(N_Z, 16, 128),
            vmem(N_Y, N_Z, 16, 128),
            vmem(4, BLOCK, 384, dtype=BF16),
            vmem(BLOCK, WIDTH, dtype=BF16),
            vmem(5, BLOCK, WIDTH),
            vmem(5, N_Y, 16, WIDTH, dtype=BF16),
            vmem(N_Z, 16, 128),
            vmem(N_Z, 16, 128, dtype=BF16),
            vmem(N_Y + 1, N_Z, 16, 128, dtype=BF16),
            vmem(N_X, 2, 8, 128),
            vmem(N_X, 8, 128),
            vmem(N_X, 8, 128),
            vmem(N_X, 8, 128),
            vmem(2, 8, 128),
            vmem(N_Y, 8, 128),
            vmem(N_Z, 8, 128),
            vmem(8, 128),
            vmem(N_Z, 8, 128),
            vmem(N_Y, 8, 128),
        ]
        + dma(4, 2) + dma(4, 4) + dma(4)
        + dma(4, 2) + dma(N_Z) + dma(N_Z) + dma(4)
        + dma(5, 4) + dma(N_Z) + dma(N_Z) + dma(4)
        + dma(4) + dma(4) + dma(4) + dma(N_Z) + dma(N_MP) + dma(N_Z) + dma(4),
        compiler_params=pltpu.CompilerParams(collective_id=1, has_side_effects=True, vmem_limit_bytes=48 << 20),
        name="layer",
    )(*(pltpu.with_memory_space_constraint(a, pltpu.HBM) for a in operands[:9]), *operands[9:])


def factor_kernel(
    mean, merged, ortho, extra, token_grad_in,
    in_update, out_update, in_error, out_error, in_right, out_right, gain_grad, table_grad, token_grad,
):
    split = 3 * WIDTH
    in_ortho, out_ortho = ortho[:, :BLOCK], ortho[:, BLOCK:]
    right = nn(in_ortho, mean[:, :split], precision=HIGH)
    in_right[...] = right
    update = tn(in_ortho, right, precision=HIGH)
    in_update[...] = update
    in_error[...] = merged[:, :split] - update
    right = nn(out_ortho, mean[:, split:], precision=HIGH)
    out_right[...] = right
    update = tn(out_ortho, right, precision=HIGH)
    out_update[...] = update
    out_error[...] = merged[:, split:] - update

    share = 1.0 / (N_Y * N_Z * N_MP)
    buckets = table_grad.shape[1]
    for head in range(HEADS):
        for c in range(CHUNKS):
            width = min(128, buckets - 128 * c)
            table_grad[head : head + 1, 128 * c : 128 * c + width] = extra[head, c : c + 1, :width] * share
    for pair in range(HEADS // 2):
        low, high = extra[2 * pair, 6:7, :], pltpu.roll(extra[2 * pair + 1, 6:7, :], 64, 1)
        lane = lax.broadcasted_iota(jnp.int32, (1, 128), 1)
        gain_grad[:, 128 * pair : 128 * (pair + 1)] = jnp.where(lane < 64, low, high) * share
    token_grad[...] = token_grad_in[...]


def factors(buckets, *operands):
    wide = jax.ShapeDtypeStruct((BLOCK, 3 * WIDTH), F32)
    thin = jax.ShapeDtypeStruct((BLOCK, WIDTH), F32)
    return pl.pallas_call(
        factor_kernel,
        out_shape=(
            wide, thin, wide, thin,
            jax.ShapeDtypeStruct((32, 3 * WIDTH), F32),
            jax.ShapeDtypeStruct((32, WIDTH), F32),
            jax.ShapeDtypeStruct((1, WIDTH), F32),
            jax.ShapeDtypeStruct((HEADS, buckets), F32),
            jax.ShapeDtypeStruct((ROWS, WIDTH), BF16),
        ),
        in_specs=[VMEM] * len(operands),
        out_specs=(VMEM,) * 9,
        compiler_params=pltpu.CompilerParams(vmem_limit_bytes=32 << 20),
        name="factors",
    )(*operands)


def shards(
    tokens,
    cotangent,
    region_ids,
    rel_bucket,
    norm_gain,
    in_weight,
    out_weight,
    bias_table,
    in_error,
    out_error,
    in_basis,
    out_basis,
):
    tok = tokens.reshape(ROWS, WIDTH)
    gain = norm_gain.reshape(1, WIDTH)
    full_in, full_out, bias, normed, flipped = gather_weights(in_weight, out_weight, bias_table, rel_bucket, tok, gain)
    token_grad, merged, mean, extra_all, ortho = layer(
        cotangent.reshape(ROWS, WIDTH), region_ids, in_error[0], out_error[0], tok, gain, rel_bucket,
        in_basis[0].T, out_basis[0].T,
        bias, normed, flipped, full_in, full_out,
    )
    in_update, out_update, in_new, out_new, in_right, out_right, gain_grad, table_grad, token_grad = factors(
        bias_table.shape[1], mean, merged, ortho, extra_all, token_grad
    )
    return (
        token_grad.reshape(tokens.shape),
        gain_grad.reshape(WIDTH),
        table_grad,
        in_update,
        out_update,
        in_new[None],
        out_new[None],
        in_right.T[None],
        out_right.T[None],
    )


def solution(mesh):
    placed = (
        P(("dp", "mp"), None, None),
        P(("dp", "mp"), None, None),
        P(("dp", "mp"), None),
        P(),
        P(),
        P("mp", None),
        P("mp", None),
        P(),
        P("dp", "mp", None),
        P("dp", "mp", None),
        P("mp", None, None),
        P("mp", None, None),
    )
    return jax.shard_map(
        shards,
        mesh=mesh,
        in_specs=placed,
        out_specs=(
            P(("dp", "mp"), None, None),
            P(),
            P(),
            P("mp", None),
            P("mp", None),
            P("dp", "mp", None),
            P("dp", "mp", None),
            P("mp", None, None),
            P("mp", None, None),
        ),
        check_vma=False,
    )
```
